32 devices in a mesh: groups: 2 (over y), vocab: 4 (over z), mp: 2 (over x), sub: 2 (over core).
Axes of the slice: x: 2, y: 2, z: 4, core: 2. Of those that a mesh axis runs over, the one named last changes fastest.
Arguments:
- previous_embedding: bfloat16 [32768, 4096], P('vocab', ('mp', 'sub')), may hold values from -6 to 6
- tile_source: int32 [32, 8], P(('groups', 'vocab')), parts along dimension 0, may hold values from 0 to 255, as said below
- tile_mask: int32 [32, 8, 128, 128], P(('groups', 'vocab')), parts along dimension 0, may hold values from 0 to 1, as said below
- row_order: int32 [4096], P(('groups', 'vocab')), parts along dimension 0, may hold values from 0 to 2047, as said below
- w_in: bfloat16 [4096, 4096], P('vocab', ('mp', 'sub')), may hold values from -0.09375 to 0.09375
- b_in: float32 [4096], P(('mp', 'sub')), may hold values from -3 to 3
- w_out: bfloat16 [4096, 4096], P(('mp', 'sub'), 'vocab'), may hold values from -0.09375 to 0.09375
- grad_out: bfloat16 [4096, 4096], P(('groups', 'vocab'), ('mp', 'sub')), parts along dimension 0, may hold values from -6 to 6
Outputs:
- grad_w_in: float32 [8192, 4096], P(('groups', 'vocab'), ('mp', 'sub')), parts along dimension 0
- grad_w_out: float32 [8192, 4096], P(('groups', 'mp', 'sub'), 'vocab'), parts along dimension 0
- grad_bias: float32 [8192], P(('groups', 'mp', 'sub')), parts along dimension 0
The draws below stay inside these ranges and needn't reach their ends.
There are 2 independent parts, one for each index of `groups`. The reference program is written for one: setup_inputs(seed, part) draws one part's arguments, and reference() takes and returns one part's arrays. A program takes and returns all parts, laid end to end along the dimension named above; an argument that names none is the same for every part. Nothing has to cross between parts.
Inputs may be any that keep to these rules, and one draw needn't show every extreme that they name: `tile_source`: old tile column c belongs to vocab index c // 64. Among the 32 slots of each aligned group of 4 target blocks, at most 16 name tiles of one vocab index, and in every group some vocab index is named exactly 16 times. Repeated tiles may occur. `tile_mask`: in every slot's tile the ones lie in exactly 64 of the 128 columns, each of which holds at least one one. Each number occurs once, and row_order[i] lies in the same aligned group of 512 rows as i.
All inputs are finite; a program needn't handle non-finite values.
Results may differ from the reference program's by a relative error of at most 0.0085.
Values may be sent and summed in bfloat16 or wider, within the bound.
No kernel may reach another device: no remote copies, remote signals or barrier semaphores. Data moves between devices by JAX's collectives and lax.ppermute only.
A program may use at most 192 MiB of HBM per device.

```python
import jax
import jax.numpy as jnp
from jax import lax

MODEL_WIDTH = 4096
OLD_VOCAB_ROWS = 32768
FF = 4096
TILE_SIZE = 128
USED = 64
KT = 8
ROWS_DEV = 512
OLD_ROWS_SHARD = 8192
ROWS = 2048
BLOCKS_DEV = 4
BLOCKS = 16
CAP = 16
N_VOCAB = 4


def draw_tile_source(key, part):
    key = jax.random.fold_in(key, 11)
    slot_count = BLOCKS_DEV * KT
    tiles_each_shard = OLD_ROWS_SHARD // TILE_SIZE

    def one_device(index):
        dev_key = jax.random.fold_in(key, index)
        key_full, key_rest, key_mix, key_tile = jax.random.split(dev_key, 4)
        full_owner = jax.random.randint(key_full, (), 0, N_VOCAB)
        free_spots = jax.random.permutation(key_rest, (N_VOCAB - 1) * CAP)[:slot_count - CAP]
        others = (free_spots // CAP).astype(jnp.int32)
        others = others + (others >= full_owner).astype(jnp.int32)
        owners = jnp.concatenate([jnp.full((CAP,), full_owner, jnp.int32), others])
        owners = jax.random.permutation(key_mix, owners)
        local_ids = jax.random.randint(key_tile, (slot_count,), 0, tiles_each_shard)
        return (owners * tiles_each_shard + local_ids).reshape(BLOCKS_DEV, KT).astype(jnp.int32)
    return jax.vmap(one_device)(jnp.arange(N_VOCAB, dtype=jnp.int32)).reshape(BLOCKS, KT)


def draw_tile_mask(key, part):
    key = jax.random.fold_in(key, 37)

    def one_slot(index):
        slot_key = jax.random.fold_in(key, index)
        key_cols, key_rows, key_extra = jax.random.split(slot_key, 3)
        allowed = jax.random.permutation(key_cols, TILE_SIZE) < USED
        forced_rows = jax.random.randint(key_rows, (TILE_SIZE,), 0, TILE_SIZE)
        forced = forced_rows[None, :] == jnp.arange(TILE_SIZE, dtype=jnp.int32)[:, None]
        extra = jax.random.randint(key_extra, (TILE_SIZE, TILE_SIZE), 0, KT * TILE_SIZE) < 5
        return (allowed[None, :] & (forced | extra)).astype(jnp.int32)
    slots = jax.vmap(one_slot)(jnp.arange(BLOCKS * KT, dtype=jnp.int32))
    return slots.reshape(BLOCKS, KT, TILE_SIZE, TILE_SIZE)


def draw_row_order(key, part):
    key = jax.random.fold_in(key, 23)

    def one_device(index):
        shuffled = jax.random.permutation(jax.random.fold_in(key, index), ROWS_DEV).astype(jnp.int32)
        return shuffled + index * ROWS_DEV
    return jax.vmap(one_device)(jnp.arange(N_VOCAB, dtype=jnp.int32)).reshape(ROWS)


def raised(values, stream_key, source, target, shards_of, factor):
    def block_of(dim):
        return (jnp.arange(values.shape[dim]) // (values.shape[dim] // shards_of)).reshape((-1,) + (1,) * (values.ndim - 1 - dim))

    near = jax.random.permutation(stream_key, shards_of)[block_of(target)]
    far = (block_of(target) + shards_of // 2) % shards_of
    return jnp.where((block_of(source) == near) | (block_of(source) == far), factor * values, values)


def levels(rng, shape, shards, least, largest):
    def one(position, parts):
        steps = jax.random.uniform(jax.random.fold_in(jax.random.fold_in(rng, 6), position), (parts,), jnp.float32, least / len(shards), largest / len(shards))
        return jnp.repeat(jnp.exp(steps), shape[position] // parts).reshape((-1,) + (1,) * (len(shape) - position - 1))

    level = one(*shards[0])
    for cut in shards[1:]:
        level = level * one(*cut)
    return level


def centred(key, shape, spread, reach, cuts=(), kind=jnp.bfloat16):
    array = jax.random.normal(key, shape, jnp.float32) * spread
    if len(cuts) > 0:
        array = levels(key, shape, cuts, -0.22, 0.18) * array
    return jnp.clip(array, min=-reach, max=reach).astype(kind)


def noise_with(own_key, shape, width, bound, cuts, heavy, kind=jnp.bfloat16):
    drawn = width * jax.random.normal(own_key, shape, jnp.float32)
    if cuts:
        drawn = drawn * levels(own_key, shape, cuts, -0.22, 0.18)
    return jnp.clip(raised(drawn, jax.random.fold_in(own_key, 3), *heavy), -bound, bound).astype(kind)


def setup_inputs(seed: int = 0, part: int = 0) -> dict:
    streams_of = jax.random.split(jax.random.key(seed), 9)
    part_keys = jax.random.split(jax.random.fold_in(streams_of[8], part), 9)
    previous_embedding = centred(streams_of[0], (OLD_VOCAB_ROWS, MODEL_WIDTH), 1.0, 6.0, ((0, 4), (1, 4)))
    tile_source = draw_tile_source(jax.random.fold_in(jax.random.fold_in(streams_of[8], part), 71), part)
    tile_mask = draw_tile_mask(jax.random.fold_in(jax.random.fold_in(streams_of[8], part), 71), part)
    row_order = draw_row_order(jax.random.fold_in(jax.random.fold_in(streams_of[8], part), 71), part)
    w_in = centred(streams_of[4], (MODEL_WIDTH, FF), MODEL_WIDTH ** -0.5, 0.09375, ((0, 4), (1, 4)))
    b_in = centred(streams_of[5], (FF,), 0.5, 3.0, ((0, 4),), jnp.float32)
    w_out = centred(streams_of[6], (FF, MODEL_WIDTH), FF ** -0.5, 0.09375, ((0, 4), (1, 4)))
    grad_out = noise_with(part_keys[7], (ROWS, MODEL_WIDTH), 1.0, 6.0, ((0, 4), (1, 4)), (0, 1, 4, 2.0))
    return dict(previous_embedding=previous_embedding, tile_source=tile_source, tile_mask=tile_mask, row_order=row_order, w_in=w_in, b_in=b_in, w_out=w_out, grad_out=grad_out)


tanh_scale = 0.7978845608028654
cubic_term = 0.044715


def gelu_parts(values):
    inner_arg = tanh_scale * (values + cubic_term * values * values * values)
    tangent = jnp.tanh(inner_arg)
    activation = 0.5 * values * (1.0 + tangent)
    act_slope = 0.5 * (1.0 + tangent) + 0.5 * values * (1.0 - tangent * tangent) * tanh_scale * (1.0 + 3.0 * cubic_term * values * values)
    return activation, act_slope


def rounded(values):
    return lax.optimization_barrier(values.astype(jnp.bfloat16)).astype(jnp.float32)


def reference(previous_embedding, tile_source, tile_mask, row_order, w_in, b_in, w_out, grad_out):
    tile_lookup = previous_embedding.reshape(OLD_VOCAB_ROWS // TILE_SIZE, TILE_SIZE, MODEL_WIDTH)

    def one_block(items):
        sources, masks = items
        tiles = tile_lookup[sources].astype(jnp.float32)
        summed = jnp.einsum("krc,kcd->rd", masks.astype(jnp.float32), tiles)
        counts = jnp.sum(masks, axis=(0, 2))
        inverse = 1.0 / jnp.maximum(counts, 1).astype(jnp.float32)
        return (summed * inverse[:, None]).astype(jnp.bfloat16)

    mixed = lax.map(one_block, (tile_source, tile_mask)).reshape(ROWS, MODEL_WIDTH)
    ordered = mixed[row_order]
    preact = jnp.dot(ordered, w_in, preferred_element_type=jnp.float32) + b_in
    activation, act_slope = gelu_parts(preact)
    hidden = activation.astype(jnp.bfloat16)
    hidden_grad = jnp.dot(grad_out, w_out.T, preferred_element_type=jnp.float32)
    pre_grad = (hidden_grad * act_slope).astype(jnp.bfloat16)
    grad_bias = jnp.sum(pre_grad.astype(jnp.float32), axis=0)

    def add_group(carry, items):
        feats, pres, cots, hids = items
        term_in = jnp.dot(feats.T, pres, preferred_element_type=jnp.float32)
        term_out = jnp.dot(hids.T, cots, preferred_element_type=jnp.float32)
        return (carry[0] + rounded(term_in), carry[1] + rounded(term_out)), None

    start_carry = (jnp.zeros((MODEL_WIDTH, FF), jnp.float32), jnp.zeros((FF, MODEL_WIDTH), jnp.float32))
    grouped = (ordered.reshape(N_VOCAB, ROWS_DEV, MODEL_WIDTH), pre_grad.reshape(N_VOCAB, ROWS_DEV, FF),
               grad_out.reshape(N_VOCAB, ROWS_DEV, MODEL_WIDTH), hidden.reshape(N_VOCAB, ROWS_DEV, FF))
    (grad_w_in, grad_w_out), unused = lax.scan(add_group, start_carry, grouped)
    return grad_w_in, grad_w_out, grad_bias
```

```python
import functools

import jax
import jax.numpy as jnp
from jax import lax
from jax.experimental import pallas as pl
from jax.experimental.pallas import tpu as pltpu
from jax.sharding import PartitionSpec as P

TILE_SIZE = 128


tanh_scale = 0.7978845608028654
cubic_term = 0.044715


def gelu_parts(values):
    inner_arg = tanh_scale * (values + cubic_term * values * values * values)
    tangent = jnp.tanh(inner_arg)
    activation = 0.5 * values * (1.0 + tangent)
    act_slope = 0.5 * (1.0 + tangent) + 0.5 * values * (1.0 - tangent * tangent) * tanh_scale * (
        1.0 + 3.0 * cubic_term * values * values
    )
    return (activation, act_slope)


TO_MIDDLE = [(0, 1), (3, 2)]
ACROSS = [(1, 2), (2, 1)]
TO_END = [(1, 0), (2, 3)]
SWAP = [(0, 1), (1, 0)]

ROW_TILE = 256
HIDDEN_CHUNK = 256
VMEM_BYTES = 56 * 1024 * 1024


def planes_fit(mesh):
    return dict(mesh.shape) == dict(groups=2, vocab=4, mp=2, sub=2)


def after(value, *others):
    return lax.optimization_barrier((value, *others))[0]


def mix_kernel(group, places, tile_ids, block_ids, *refs):
    tiles, (own_masks, sibling_masks, out, total) = refs[:places], refs[places:]
    total[...] = jnp.zeros_like(total)
    for place in range(places):
        half = places // 2
        mask = own_masks[0, place] if place < half else sibling_masks[0, place - half]
        start = pl.multiple_of(block_ids[group * places + place] * TILE_SIZE, TILE_SIZE)
        total[pl.ds(start, TILE_SIZE), :] += jnp.dot(mask, tiles[place][0], preferred_element_type=jnp.float32)
    out[...] = total[...].astype(out.dtype)


def mix_group(group, rows, tile_ids, block_ids, tile_lookup, own_masks, sibling_masks):
    half = own_masks.shape[1]
    places = 2 * half
    columns = tile_lookup.shape[2]

    def tile_spec(place):
        return pl.BlockSpec((1, TILE_SIZE, columns), lambda i, ids, blocks: (ids[group * places + place], 0, 0))

    mask_spec = pl.BlockSpec((1, half, TILE_SIZE, TILE_SIZE), lambda i, ids, blocks: (group, 0, 0, 0))
    return pl.pallas_call(
        functools.partial(mix_kernel, group, places),
        out_shape=jax.ShapeDtypeStruct((rows, columns), jnp.bfloat16),
        grid_spec=pltpu.PrefetchScalarGridSpec(
            num_scalar_prefetch=2,
            grid=(1,),
            in_specs=[tile_spec(place) for place in range(places)] + [mask_spec] * 2,
            out_specs=pl.BlockSpec((rows, columns), lambda i, ids, blocks: (0, 0)),
            scratch_shapes=[pltpu.VMEM((rows, columns), jnp.float32)],
        ),
        compiler_params=pltpu.CompilerParams(vmem_limit_bytes=VMEM_BYTES),
        cost_estimate=pl.CostEstimate(
            flops=2 * places * TILE_SIZE * TILE_SIZE * columns,
            bytes_accessed=2 * places * TILE_SIZE * columns + 2 * rows * columns,
            transcendentals=0,
        ),
        name=f"mix_group_{group}",
    )(tile_ids, block_ids, *([tile_lookup] * places), own_masks, sibling_masks)


def chunk_kernel(scalars, features, cotangent, in_own, in_end, in_far, in_far_half, out_own, out_end, out_far, out_far_half,
                 bias, grad_in, grad_in_end, grad_out, grad_out_end, grad_bias, in_all, out_all, sum_in, sum_out, sum_bias):
    step = pl.program_id(0)
    own, part = scalars[0], scalars[1]
    width = in_own.shape[0]

    @pl.when(step == 0)
    def _():
        sum_in[...] = jnp.zeros_like(sum_in)
        sum_out[...] = jnp.zeros_like(sum_out)
        sum_bias[...] = jnp.zeros_like(sum_bias)
        in_all[own] = in_own[...]
        in_all[own ^ 1] = in_end[...]
        out_all[own] = out_own[...]
        out_all[own ^ 1] = out_end[...]
        in_half, out_half = in_far.shape[1], out_far.shape[1]
        for piece, where in ((0, 3), (1, 2)):
            for source_in, source_out, half in ((in_far, out_far, part), (in_far_half, out_far_half, 1 - part)):
                in_all[own ^ where, pl.ds(pl.multiple_of(half * in_half, in_half), in_half), :] = source_in[piece]
                out_all[own ^ where, pl.ds(pl.multiple_of(half * out_half, out_half), out_half), :] = source_out[piece]

    preact = bias[...] + jnp.zeros((features.shape[2], in_own.shape[1]), jnp.float32)
    hidden_grad = jnp.zeros_like(preact)
    for k in range(features.shape[1]):
        preact += jnp.dot(features[0, k], in_all[k], preferred_element_type=jnp.float32)
        hidden_grad += lax.dot_general(
            cotangent[0, k], out_all[k], (((1,), (1,)), ((), ())), preferred_element_type=jnp.float32
        )
    activation, act_slope = gelu_parts(preact)
    hidden = activation.astype(jnp.bfloat16)
    pre_grad = (hidden_grad * act_slope).astype(jnp.bfloat16)
    sum_bias[...] += jnp.sum(pre_grad.astype(jnp.float32), axis=0, keepdims=True)
    over_rows = (((0,), (0,)), ((), ()))
    for j in range(2):
        sum_in[j] += lax.dot_general(pre_grad, features[0, own ^ j], over_rows, preferred_element_type=jnp.float32)
        sum_out[j] += lax.dot_general(hidden, cotangent[0, own ^ j], over_rows, preferred_element_type=jnp.float32)

    @pl.when(step == pl.num_programs(0) - 1)
    def _():
        grad_in[...] = sum_in[0].T
        grad_in_end[...] = sum_in[1].T.astype(jnp.bfloat16)
        grad_out[...] = sum_out[0]
        grad_out_end[...] = sum_out[1].astype(jnp.bfloat16)
        grad_bias[...] = sum_bias[...]


def hidden_chunk(chunk, scalars, features, cotangent, w_in, w_out, moved_in, moved_out, bias):
    groups, pieces, rows, width = features.shape
    tiles = rows // ROW_TILE
    size = HIDDEN_CHUNK

    def whole(array):
        return pl.BlockSpec(array.shape, lambda t, s: (0,) * array.ndim)

    row_block = (1, pieces, ROW_TILE, width)
    in_specs = [
        pl.BlockSpec(row_block, lambda t, s: (t // tiles, 0, t % tiles, 0)),
        pl.BlockSpec(row_block, lambda t, s: (s[2] ^ (t // tiles), 0, t % tiles, 0)),
        pl.BlockSpec((width, size), lambda t, s: (0, chunk)),
        *[whole(array) for array in moved_in],
        pl.BlockSpec((size, width), lambda t, s: (chunk, 0)),
        *[whole(array) for array in moved_out],
        pl.BlockSpec((1, size), lambda t, s: (0, chunk)),
    ]
    shapes = [
        jax.ShapeDtypeStruct((width, size), jnp.float32),
        jax.ShapeDtypeStruct((width, size), jnp.bfloat16),
        jax.ShapeDtypeStruct((size, width), jnp.float32),
        jax.ShapeDtypeStruct((size, width), jnp.bfloat16),
        jax.ShapeDtypeStruct((1, size), jnp.float32),
    ]
    return pl.pallas_call(
        chunk_kernel,
        out_shape=shapes,
        grid_spec=pltpu.PrefetchScalarGridSpec(
            num_scalar_prefetch=1,
            grid=(groups * tiles,),
            in_specs=in_specs,
            out_specs=[pl.BlockSpec(shape.shape, lambda t, s: (0, 0)) for shape in shapes],
            scratch_shapes=[
                pltpu.VMEM((pieces, width, size), jnp.bfloat16),
                pltpu.VMEM((pieces, size, width), jnp.bfloat16),
                pltpu.VMEM((2, size, width), jnp.float32),
                pltpu.VMEM((2, size, width), jnp.float32),
                pltpu.VMEM((1, size), jnp.float32),
            ],
        ),
        compiler_params=pltpu.CompilerParams(vmem_limit_bytes=VMEM_BYTES),
        cost_estimate=pl.CostEstimate(
            flops=2 * 2 * groups * rows * (pieces + 2) * width * size,
            bytes_accessed=2 * 2 * groups * pieces * rows * width,
            transcendentals=groups * rows * size,
        ),
        name=f"hidden_chunk_{chunk}",
    )(scalars, features, cotangent, w_in, *moved_in, w_out, *moved_out, bias)


def in_plane(piece):
    across = lax.ppermute(piece, "mp", SWAP)
    return [piece, lax.ppermute(piece, "sub", SWAP), across, lax.ppermute(across, "sub", SWAP)]


def middle_planes(previous_embedding, tile_source, tile_mask, row_order, w_in, b_in, w_out, grad_out):
    plane, part, core = lax.axis_index("vocab"), lax.axis_index("groups"), lax.axis_index("sub")
    column = 2 * lax.axis_index("mp") + core
    planes = lax.axis_size("vocab")
    blocks, slots_per = tile_source.shape
    total_slots = blocks * slots_per
    tiles_here = previous_embedding.shape[0] // TILE_SIZE
    columns = previous_embedding.shape[1]
    tile_lookup = previous_embedding.reshape(tiles_here, TILE_SIZE, columns)
    rows = row_order.shape[0]
    places = 2 * total_slots // planes
    half = places // 2

    all_source = lax.all_gather(tile_source.reshape(1, -1), "vocab", axis=0, tiled=True)
    slot_ids = jnp.arange(total_slots)
    earlier = slot_ids[None, :] < slot_ids[:, None]

    def owners_and_places(sources):
        owner = sources // tiles_here
        same = owner[..., None, :] == owner[..., :, None]
        return owner, jnp.sum(jnp.where(earlier & same, 1, 0), axis=-1).astype(jnp.int32)

    owner, position = owners_and_places(tile_source.reshape(-1))
    my_places = core * half + jnp.arange(half)
    hit = (owner[:, None, None] == jnp.arange(planes)[None, :, None]) & (
        position[:, None, None] == my_places[None, None, :]
    )
    slot_of = jnp.sum(jnp.where(hit, slot_ids[:, None, None], 0), axis=0)
    filled = jnp.any(hit, axis=0)
    sent = jnp.take(tile_mask.reshape(total_slots, TILE_SIZE, TILE_SIZE), slot_of.reshape(-1), axis=0)
    sent = jnp.where(filled.reshape(-1)[:, None, None], sent, 0).astype(jnp.bfloat16)
    sent = sent.reshape(planes, half, TILE_SIZE, TILE_SIZE)
    own_masks = lax.all_to_all(sent, "vocab", split_axis=0, concat_axis=0, tiled=True)
    sibling_masks = lax.ppermute(own_masks, "sub", SWAP)

    all_owner, all_position = owners_and_places(all_source)
    both_places = jnp.concatenate([my_places, (1 - core) * half + jnp.arange(half)])
    mine = (all_owner == plane)[:, :, None] & (all_position[:, :, None] == both_places[None, None, :])
    tile_ids = jnp.sum(jnp.where(mine, (all_source % tiles_here)[:, :, None], 0), axis=1).reshape(-1)
    block_ids = jnp.sum(jnp.where(mine, (slot_ids // slots_per)[None, :, None], 0), axis=1).reshape(-1)

    counts = jnp.sum(tile_mask, axis=(1, 3)).reshape(1, rows)
    inverse = 1.0 / jnp.maximum(counts, 1).astype(jnp.float32)
    all_inverse = lax.all_gather(inverse, "vocab", axis=0, tiled=True)

    placed = (row_order % rows)[None, :] == jnp.arange(rows)[:, None]
    cotangent = jnp.dot(placed.astype(jnp.bfloat16), grad_out, preferred_element_type=jnp.float32).astype(jnp.bfloat16)
    cot_end = lax.ppermute(cotangent, "vocab", TO_MIDDLE)
    cot_far = lax.ppermute(after(cotangent, own_masks), "vocab", ACROSS)
    cot_far_end = lax.ppermute(after(cot_end, own_masks), "vocab", ACROSS)
    cotangents = jnp.stack([jnp.stack(in_plane(piece)) for piece in (cotangent, cot_end, cot_far_end, cot_far)])

    features = []
    arrived, summed = [], []
    for group in range(planes):
        partial = mix_group(group, rows, tile_ids, block_ids, tile_lookup, own_masks, sibling_masks)
        from_end = lax.ppermute(partial, "vocab", TO_MIDDLE)
        arrived.append(from_end)
        side = (partial.astype(jnp.float32) + from_end.astype(jnp.float32)).astype(jnp.bfloat16)
        other = lax.ppermute(side, "vocab", ACROSS)
        summed.append(other)
        mixed = (side.astype(jnp.float32) + other.astype(jnp.float32)) * all_inverse[group][:, None]
        features.append(jnp.stack(in_plane(mixed.astype(jnp.bfloat16))))
    features = jnp.stack(features)

    hidden_units = w_in.shape[1]
    chunks = hidden_units // HIDDEN_CHUNK
    in_half, out_half = w_in.shape[0] // 2, HIDDEN_CHUNK // 2
    scalars = jnp.stack([plane ^ column, part, plane]).astype(jnp.int32)
    bias = b_in.reshape(1, -1)
    is_middle = (plane == 1) | (plane == 2)
    before_end = [cot_end, arrived[2], arrived[3], None]
    before_far = [summed[1], summed[2], summed[3], None]
    grad_w_in, grad_w_out, grad_bias = [], [], []
    for chunk in range(chunks):
        in_here = w_in[:, chunk * HIDDEN_CHUNK : (chunk + 1) * HIDDEN_CHUNK]
        out_here = w_out[chunk * HIDDEN_CHUNK : (chunk + 1) * HIDDEN_CHUNK]
        gate = before_end[chunk] if chunk < 3 else in_end
        in_end = lax.ppermute(after(in_here, gate), "vocab", TO_MIDDLE)
        out_end = lax.ppermute(after(out_here, gate), "vocab", TO_MIDDLE)

        def my_half(array, size):
            return lax.dynamic_slice_in_dim(array, part * size, size, axis=0)

        in_halves = jnp.stack([my_half(in_here, in_half), my_half(in_end, in_half)])
        out_halves = jnp.stack([my_half(out_here, out_half), my_half(out_end, out_half)])
        gate = before_far[chunk] if chunk < 3 else in_far
        in_far = lax.ppermute(after(in_halves, gate), "vocab", ACROSS)
        out_far = lax.ppermute(after(out_halves, gate), "vocab", ACROSS)
        in_far_half = lax.ppermute(in_far, "groups", SWAP)
        out_far_half = lax.ppermute(out_far, "groups", SWAP)
        own_in, end_in, own_out, end_out, chunk_bias = hidden_chunk(
            chunk, scalars, features, cotangents, w_in, w_out,
            (in_end, in_far, in_far_half), (out_end, out_far, out_far_half), bias,
        )
        got_in = lax.ppermute(end_in, "vocab", TO_END)
        got_out = lax.ppermute(end_out, "vocab", TO_END)
        grad_w_in.append(jnp.where(is_middle, own_in, got_in.astype(jnp.float32)))
        grad_w_out.append(jnp.where(is_middle, own_out, got_out.astype(jnp.float32)))
        grad_bias.append(chunk_bias)
    grad_bias = jnp.concatenate(grad_bias, axis=1)
    got_bias = lax.ppermute(grad_bias, "vocab", TO_END)
    grad_bias = jnp.where(is_middle, grad_bias, got_bias).reshape(-1)
    return (jnp.concatenate(grad_w_in, axis=1), jnp.concatenate(grad_w_out, axis=0), grad_bias)


def gathered(previous_embedding, tile_source, tile_mask, row_order, w_in, b_in, w_out, grad_out):
    groups = lax.axis_size("vocab")
    blocks, slots_per = tile_source.shape
    tiles_here = previous_embedding.shape[0] // TILE_SIZE
    columns = previous_embedding.shape[1]
    flat_source = tile_source.reshape(-1)
    owner_dev = flat_source // tiles_here
    local_tile = flat_source % tiles_here
    total_slots = flat_source.shape[0]
    capacity = max(2, 2 * total_slots // groups)
    slot_ids = jnp.arange(total_slots)
    earlier = slot_ids[None, :] < slot_ids[:, None]
    same_owner = owner_dev[None, :] == owner_dev[:, None]
    position = jnp.sum(jnp.where(earlier & same_owner, 1, 0), axis=1).astype(jnp.int32)
    owner_hit = owner_dev[:, None] == jnp.arange(groups)[None, :]
    place_hit = position[:, None] == jnp.arange(capacity)[None, :]
    placed = owner_hit[:, :, None] & place_hit[:, None, :]
    slot_index = owner_dev * capacity + position
    mask_values = tile_mask.astype(jnp.bfloat16)
    requests = jnp.sum(jnp.where(placed, local_tile[:, None, None], 0), axis=0)
    tile_lookup = previous_embedding.reshape(tiles_here, TILE_SIZE, columns)
    found_tiles = jnp.take(
        tile_lookup,
        lax.all_to_all(requests, "vocab", split_axis=0, concat_axis=0, tiled=True),
        axis=0,
    )
    arrived = lax.all_to_all(found_tiles, "vocab", split_axis=0, concat_axis=0, tiled=True)
    picked = arrived.reshape(groups * capacity, TILE_SIZE, columns)[slot_index]
    picked = picked.reshape(blocks, slots_per, TILE_SIZE, columns)
    summed = jnp.einsum("bkrc,bkcd->brd", mask_values, picked, preferred_element_type=jnp.float32)
    counts = jnp.sum(tile_mask, axis=(1, 3))
    inverse = 1.0 / jnp.maximum(counts, 1).astype(jnp.float32)
    mixed = (summed * inverse[:, :, None]).astype(jnp.bfloat16).reshape(blocks * TILE_SIZE, columns)
    rows_here = mixed.shape[0]
    ordered = mixed[row_order % rows_here]
    w_in_full = lax.all_gather(w_in, "vocab", axis=0, tiled=True)
    features = lax.all_gather(ordered, ("mp", "sub"), axis=1, tiled=True)
    preact = jnp.dot(features, w_in_full, preferred_element_type=jnp.float32) + b_in
    activation, act_slope = gelu_parts(preact)
    hidden = activation.astype(jnp.bfloat16)
    w_out_full = lax.all_gather(w_out, "vocab", axis=1, tiled=True)
    cotangent = lax.all_gather(grad_out, ("mp", "sub"), axis=1, tiled=True)
    hidden_grad = lax.dot_general(
        cotangent, w_out_full, (((1,), (1,)), ((), ())), preferred_element_type=jnp.float32
    )
    pre_grad = (hidden_grad * act_slope).astype(jnp.bfloat16)
    grad_bias = lax.psum(jnp.sum(pre_grad.astype(jnp.float32), axis=0), "vocab")
    grad_w_in = lax.psum_scatter(
        lax.dot_general(
            features, pre_grad, (((0,), (0,)), ((), ())), preferred_element_type=jnp.float32
        ).astype(jnp.bfloat16),
        "vocab",
        scatter_dimension=0,
        tiled=True,
    ).astype(jnp.float32)
    grad_w_out = (
        lax.psum_scatter(
            lax.dot_general(
                cotangent, hidden, (((0,), (0,)), ((), ())), preferred_element_type=jnp.float32
            ).astype(jnp.bfloat16),
            "vocab",
            scatter_dimension=0,
            tiled=True,
        )
        .astype(jnp.float32)
        .T
    )
    return (grad_w_in, grad_w_out, grad_bias)


def solution(mesh):
    placed = (
        P("vocab", ("mp", "sub")),
        P(("groups", "vocab"), None),
        P(("groups", "vocab"), None, None, None),
        P(("groups", "vocab")),
        P("vocab", ("mp", "sub")),
        P(("mp", "sub")),
        P(("mp", "sub"), "vocab"),
        P(("groups", "vocab"), ("mp", "sub")),
    )
    return jax.shard_map(
        middle_planes if planes_fit(mesh) else gathered,
        mesh=mesh,
        in_specs=placed,
        out_specs=(
            P(("groups", "vocab"), ("mp", "sub")),
            P(("groups", "mp", "sub"), "vocab"),
            P(("groups", "mp", "sub")),
        ),
        check_vma=False,
    )
```

```python
import functools

import jax
import jax.numpy as jnp
from jax import lax
from jax.experimental import pallas as pl
from jax.experimental.pallas import tpu as pltpu
from jax.sharding import PartitionSpec as P

TILE_SIZE = 128


tanh_scale = 0.7978845608028654
cubic_term = 0.044715


def gelu_parts(values):
    inner_arg = tanh_scale * (values + cubic_term * values * values * values)
    tangent = jnp.tanh(inner_arg)
    activation = 0.5 * values * (1.0 + tangent)
    act_slope = 0.5 * (1.0 + tangent) + 0.5 * values * (1.0 - tangent * tangent) * tanh_scale * (
        1.0 + 3.0 * cubic_term * values * values
    )
    return (activation, act_slope)


TO_MIDDLE = [(0, 1), (3, 2)]
ACROSS = [(1, 2), (2, 1)]
TO_END = [(1, 0), (2, 3)]
SWAP = [(0, 1), (1, 0)]

ROW_TILE = 512
AHEAD = 1
HIDDEN_CHUNK = 256
HEADER_ROWS = 16
BIAS_ROWS = 16
VMEM_BYTES = 60 * 1024 * 1024


def planes_fit(mesh):
    return dict(mesh.shape) == dict(groups=2, vocab=4, mp=2, sub=2)


def gated(values, results):
    return lax.optimization_barrier((tuple(values), tuple(results)))[0]


def mix_kernel(group, places, tile_ids, block_ids, *refs):
    tiles, (own_masks, sibling_masks, out, total) = refs[:places], refs[places:]
    total[...] = jnp.zeros_like(total)
    half = places // 2
    for place in range(places):
        masks = own_masks if place < half else sibling_masks
        mask = masks[0, (place % half) * TILE_SIZE : (place % half + 1) * TILE_SIZE, :]
        start = pl.multiple_of(block_ids[group * places + place] * TILE_SIZE, TILE_SIZE)
        total[pl.ds(start, TILE_SIZE), :] += jnp.dot(mask, tiles[place][0], preferred_element_type=jnp.float32)
    out[...] = total[...].astype(out.dtype)


def mix_group(group, rows, places, tile_ids, block_ids, tile_lookup, own_masks, sibling_masks):
    columns = tile_lookup.shape[2]

    def tile_spec(place):
        return pl.BlockSpec((1, TILE_SIZE, columns), lambda i, ids, blocks: (ids[group * places + place], 0, 0))

    mask_spec = pl.BlockSpec((1,) + own_masks.shape[1:], lambda i, ids, blocks: (group, 0, 0))
    return pl.pallas_call(
        functools.partial(mix_kernel, group, places),
        out_shape=jax.ShapeDtypeStruct((rows, columns), jnp.bfloat16),
        grid_spec=pltpu.PrefetchScalarGridSpec(
            num_scalar_prefetch=2,
            grid=(1,),
            in_specs=[tile_spec(place) for place in range(places)] + [mask_spec] * 2,
            out_specs=pl.BlockSpec((rows, columns), lambda i, ids, blocks: (0, 0)),
            scratch_shapes=[pltpu.VMEM((rows, columns), jnp.float32)],
        ),
        compiler_params=pltpu.CompilerParams(vmem_limit_bytes=VMEM_BYTES),
        cost_estimate=pl.CostEstimate(
            flops=2 * places * TILE_SIZE * TILE_SIZE * columns,
            bytes_accessed=2 * places * TILE_SIZE * columns + 2 * rows * columns,
            transcendentals=0,
        ),
        name=f"mix_group_{group}",
    )(tile_ids, block_ids, *([tile_lookup] * places), own_masks, sibling_masks)


def chunk_kernel(pieces, far_places, scalars, *refs):
    feature_refs = [refs[g * pieces : (g + 1) * pieces] for g in range(4)]
    cotangent_refs = [refs[(4 + g) * pieces : (5 + g) * pieces] for g in range(4)]
    (own_pack, *fars, bias, grad_in, grad_out, end_grads, grad_bias,
     features, cotangent, in_all, out_all, sum_in, sum_out, sum_bias, sems, weight_sems) = refs[8 * pieces :]
    fars = [far if place is None else far.at[place] for far, place in zip(fars, far_places)]
    own, part, plane = scalars[0], scalars[1], scalars[2]
    size = in_all.shape[1]
    rows, width = feature_refs[0][0].shape
    tiles = rows // ROW_TILE

    def weights(source, target, k, kind):
        target = target.at[pl.ds(pl.multiple_of((own ^ k) * width, width), width)]
        return pltpu.make_async_copy(source, target, weight_sems.at[kind, k])

    for kind, target in ((0, in_all), (1, out_all)):
        weights(own_pack.at[pl.ds(kind * width, width)], target, 0, kind).start()
    for half in range(2):

        @pl.when(part == half)
        def _():
            for i, k in ((0, 3), (1, 2), (2, 1)):
                weights(fars[3 * half + i], in_all, k, 0).start()
                weights(fars[3 - 3 * half + i], out_all, k, 1).start()

    def move(source, target, kind, step, tile, k):
        from_rows = pl.ds(pl.multiple_of(tile * ROW_TILE, ROW_TILE), ROW_TILE)
        to_rows = pl.ds(pl.multiple_of(step * ROW_TILE, ROW_TILE), ROW_TILE)
        return pltpu.make_async_copy(
            source.at[from_rows], target.at[to_rows, pl.ds(k * width, width)], sems.at[kind, step, k]
        )

    def fetch(step):
        group, tile = step // tiles, step % tiles
        for i in range(4):

            @pl.when(group == i)
            def _():
                for k in range(pieces):
                    move(feature_refs[i][k], features, 0, step, tile, k).start()

            @pl.when((plane ^ group) == i)
            def _():
                for k in range(pieces):
                    move(cotangent_refs[i][k], cotangent, 1, step, tile, k).start()

    for step in range(AHEAD):
        fetch(step)
    sum_in[...] = jnp.zeros_like(sum_in)
    sum_out[...] = jnp.zeros_like(sum_out)
    sum_bias[...] = jnp.zeros_like(sum_bias)
    for k in range(pieces):
        weights(fars[0], in_all, k, 0).wait()
        weights(fars[0], out_all, k, 1).wait()

    @pl.loop(0, 4 * tiles)
    def _(step):
        @pl.when(step + AHEAD < 4 * tiles)
        def _():
            fetch(step + AHEAD)

        here = pl.ds(pl.multiple_of(step * ROW_TILE, ROW_TILE), ROW_TILE)
        for k in range(pieces):
            move(feature_refs[0][k], features, 0, step, 0, k).wait()
            move(cotangent_refs[0][k], cotangent, 1, step, 0, k).wait()
        preact = bias[...] + jnp.dot(features[here, :], in_all[...], preferred_element_type=jnp.float32)
        hidden_grad = jnp.dot(cotangent[here, :], out_all[...], preferred_element_type=jnp.float32)
        activation, act_slope = gelu_parts(preact)
        hidden = activation.astype(jnp.bfloat16)
        pre_grad = (hidden_grad * act_slope).astype(jnp.bfloat16)
        sum_bias[...] += jnp.sum(pre_grad.astype(jnp.float32), axis=0, keepdims=True)
        hidden, pre_grad = hidden.T, pre_grad.T
        for j in range(2):
            columns = pl.ds(pl.multiple_of((own ^ j) * width, width), width)
            sum_in[j] += jnp.dot(pre_grad, features[here, columns], preferred_element_type=jnp.float32)
            sum_out[j] += jnp.dot(hidden, cotangent[here, columns], preferred_element_type=jnp.float32)

    grad_in[...] = sum_in[0].T
    grad_out[...] = sum_out[0]
    end_grads[:width, :] = sum_in[1].T.astype(jnp.bfloat16)
    for q in range(width // size):
        end_grads[width + q * size : width + (q + 1) * size, :] = sum_out[1, :, q * size : (q + 1) * size].astype(jnp.bfloat16)
    grad_bias[...] = sum_bias[...]
    part_rows = lax.broadcasted_iota(jnp.int32, (BIAS_ROWS, size), 0)
    rest = sum_bias[...]
    parts = jnp.zeros((BIAS_ROWS, size), jnp.float32)
    for i in range(3):
        rounded = rest.astype(jnp.bfloat16).astype(jnp.float32)
        parts = jnp.where(part_rows == i, rounded, parts)
        rest = rest - rounded
    end_grads[2 * width :, :] = parts.astype(jnp.bfloat16)


def hidden_chunk(chunk, scalars, features, cotangents, own_pack, fars, bias):
    groups, pieces = len(features), len(features[0])
    rows, width = features[0][0].shape
    size = HIDDEN_CHUNK
    flat = [piece for group in features for piece in group] + [piece for group in cotangents for piece in group]
    flat += [own_pack] + [array for array, _ in fars]

    def whole(array):
        return pl.BlockSpec(array.shape, lambda i, s: (0,) * array.ndim)

    shapes = [
        jax.ShapeDtypeStruct((width, size), jnp.float32),
        jax.ShapeDtypeStruct((size, width), jnp.float32),
        jax.ShapeDtypeStruct((2 * width + BIAS_ROWS, size), jnp.bfloat16),
        jax.ShapeDtypeStruct((1, size), jnp.float32),
    ]
    return pl.pallas_call(
        functools.partial(chunk_kernel, pieces, [place for _, place in fars]),
        out_shape=shapes,
        grid_spec=pltpu.PrefetchScalarGridSpec(
            num_scalar_prefetch=1,
            grid=(1,),
            in_specs=[pl.BlockSpec(memory_space=pl.ANY)] * len(flat) + [pl.BlockSpec((1, size), lambda i, s: (0, chunk))],
            out_specs=[whole(shape) for shape in shapes],
            scratch_shapes=[
                pltpu.VMEM((groups * rows, pieces * width), jnp.bfloat16),
                pltpu.VMEM((groups * rows, pieces * width), jnp.bfloat16),
                pltpu.VMEM((pieces * width, size), jnp.bfloat16),
                pltpu.VMEM((pieces * width, size), jnp.bfloat16),
                pltpu.VMEM((2, size, width), jnp.float32),
                pltpu.VMEM((2, size, width), jnp.float32),
                pltpu.VMEM((1, size), jnp.float32),
                pltpu.SemaphoreType.DMA((2, groups * rows // ROW_TILE, pieces)),
                pltpu.SemaphoreType.DMA((2, pieces)),
            ],
        ),
        compiler_params=pltpu.CompilerParams(vmem_limit_bytes=VMEM_BYTES),
        cost_estimate=pl.CostEstimate(
            flops=2 * 2 * groups * rows * (pieces + 2) * width * size,
            bytes_accessed=2 * 2 * groups * pieces * rows * width,
            transcendentals=groups * rows * size,
        ),
        name=f"hidden_chunk_{chunk}",
    )(scalars, *flat, bias)


def pack_kernel(half, blocks, slot_of, filled, masks, numbers, sent):
    slots_per = masks.shape[0] // blocks
    planes = sent.shape[0]

    @pl.loop(0, planes * half)
    def _(place):
        row = pl.multiple_of(lax.rem(place, half) * TILE_SIZE, TILE_SIZE)
        sent[place // half, pl.ds(row, TILE_SIZE), :] = (masks[slot_of[place]] * filled[place]).astype(sent.dtype)

    row_ids = lax.broadcasted_iota(jnp.int32, (HEADER_ROWS, TILE_SIZE), 0)
    ones = jnp.ones((HEADER_ROWS, TILE_SIZE), jnp.bfloat16)
    header = jnp.zeros((HEADER_ROWS, TILE_SIZE), jnp.float32)
    for block in range(blocks):
        total = masks[block * slots_per]
        for slot in range(1, slots_per):
            total += masks[block * slots_per + slot]
        counts = lax.dot_general(
            ones, total.astype(jnp.bfloat16), (((1,), (1,)), ((), ())), preferred_element_type=jnp.float32
        ).astype(jnp.int32)
        header = jnp.where(row_ids == 1 + block, (counts // TILE_SIZE).astype(jnp.float32), header)
        header = jnp.where(row_ids == 1 + blocks + block, (counts % TILE_SIZE).astype(jnp.float32), header)
    for plane in range(planes):
        own_numbers = numbers[plane : plane + 1, :].astype(jnp.float32)
        sent[plane, half * TILE_SIZE :, :] = jnp.where(row_ids == 0, own_numbers, header).astype(sent.dtype)


def pack_masks(slot_of, filled, masks, numbers, blocks):
    planes, half = slot_of.shape
    shape = jax.ShapeDtypeStruct((planes, half * TILE_SIZE + HEADER_ROWS, TILE_SIZE), jnp.bfloat16)
    return pl.pallas_call(
        functools.partial(pack_kernel, half, blocks),
        out_shape=shape,
        grid_spec=pltpu.PrefetchScalarGridSpec(
            num_scalar_prefetch=2,
            grid=(1,),
            in_specs=[
                pl.BlockSpec(masks.shape, lambda i, s, f: (0, 0, 0)),
                pl.BlockSpec(numbers.shape, lambda i, s, f: (0, 0)),
            ],
            out_specs=pl.BlockSpec(shape.shape, lambda i, s, f: (0, 0, 0)),
        ),
        compiler_params=pltpu.CompilerParams(vmem_limit_bytes=VMEM_BYTES),
        name="pack_masks",
    )(slot_of.reshape(-1), filled.astype(jnp.int32).reshape(-1), masks, numbers)


def middle_planes(previous_embedding, tile_source, tile_mask, row_order, w_in, b_in, w_out, grad_out):
    plane, part, core = lax.axis_index("vocab"), lax.axis_index("groups"), lax.axis_index("sub")
    column = 2 * lax.axis_index("mp") + core
    planes = lax.axis_size("vocab")
    blocks, slots_per = tile_source.shape
    total_slots = blocks * slots_per
    tiles_here = previous_embedding.shape[0] // TILE_SIZE
    columns = previous_embedding.shape[1]
    tile_lookup = previous_embedding.reshape(tiles_here, TILE_SIZE, columns)
    rows = row_order.shape[0]
    places = 2 * total_slots // planes
    half = places // 2
    bf16, f32 = jnp.bfloat16, jnp.float32

    def to_middle(array):
        return lax.ppermute(array, "vocab", TO_MIDDLE)

    def across(array):
        return lax.ppermute(array, "vocab", ACROSS)

    def to_end(array):
        return lax.ppermute(array, "vocab", TO_END)

    def swap_x(array):
        return lax.ppermute(array, "mp", SWAP)

    def swap_y(array):
        return lax.ppermute(array, "groups", SWAP)

    def swap_core(array):
        return lax.ppermute(array, "sub", SWAP)

    source = tile_source.reshape(-1)
    owner = source // tiles_here
    slot_ids = jnp.arange(total_slots)
    earlier = slot_ids[None, :] < slot_ids[:, None]
    position = jnp.sum(jnp.where(earlier & (owner[None, :] == owner[:, None]), 1, 0), axis=1)
    my_places = core * half + jnp.arange(half)
    hit = (owner[:, None, None] == jnp.arange(planes)[None, :, None]) & (
        position[:, None, None] == my_places[None, None, :]
    )
    slot_of = jnp.sum(jnp.where(hit, slot_ids[:, None, None], 0), axis=0)
    filled = jnp.any(hit, axis=0)
    numbers = jnp.concatenate(
        [
            jnp.sum(jnp.where(hit, (source % tiles_here)[:, None, None], 0), axis=0),
            jnp.sum(jnp.where(hit, (slot_ids // slots_per)[:, None, None], 0), axis=0),
        ],
        axis=1,
    )
    numbers = jnp.pad(numbers, ((0, 0), (0, TILE_SIZE - 2 * half)))
    masks = tile_mask.reshape(total_slots, TILE_SIZE, TILE_SIZE)
    sent = pack_masks(slot_of, filled, masks, numbers, blocks)

    placed = (row_order % rows)[None, :] == jnp.arange(rows)[:, None]
    cot = jnp.dot(placed.astype(bf16), grad_out, preferred_element_type=f32).astype(bf16)

    hidden_units, width = w_out.shape
    size = HIDDEN_CHUNK
    chunks = hidden_units // size
    packs = []
    for chunk in range(chunks):
        here = slice(chunk * size, (chunk + 1) * size)
        packs.append(jnp.concatenate([w_in[:, here], w_out[here].T], axis=0))

    def my_half(pack):
        return lax.dynamic_slice_in_dim(pack, part * width, width, axis=0)

    def both(a, b):
        return (a.astype(f32) + b.astype(f32)).astype(bf16)

    def mixed_of(group, side, other):
        return ((side.astype(f32) + other.astype(f32)) * all_inverse[group][:, None]).astype(bf16)

    def partial_of(group, ids):
        return mix_group(group, rows, places, ids, block_ids, tile_lookup, masks, sibling)

    def numbers_of(array):
        header = array[:, half * TILE_SIZE, : 2 * half].astype(jnp.int32)
        return header[:, :half], header[:, half:]

    own01 = jnp.stack([my_half(packs[0]), my_half(packs[1])])
    own23 = jnp.stack([my_half(packs[2]), my_half(packs[3])])
    got = lax.all_to_all(sent, "vocab", split_axis=0, concat_axis=0, tiled=True)
    cot_x = swap_x(cot)

    masks, cot, cot_x, own01, own23 = gated((got, cot, cot_x, own01, own23), ())
    sibling = swap_core(masks)
    cot_far = across(cot)
    r01 = across(own01)
    cot_end = to_middle(cot)
    cot_s, cot_xs = swap_core(cot), swap_core(cot_x)
    own_numbers, sibling_numbers = numbers_of(masks), numbers_of(sibling)
    tile_ids, block_ids = (jnp.concatenate(pair, axis=1).reshape(-1) for pair in zip(own_numbers, sibling_numbers))
    first = half * TILE_SIZE + 1
    count_high, count_low = (masks[:, first + i * blocks : first + (i + 1) * blocks].astype(f32) for i in range(2))
    all_inverse = (1.0 / jnp.maximum(count_high * TILE_SIZE + count_low, 1.0)).reshape(planes, rows)
    p0 = partial_of(0, tile_ids)

    p0, cot_end, cot_far, ids = gated((p0, cot_end, cot_far, tile_ids), (cot_s, cot_xs, all_inverse))
    cot_far_end = across(cot_end)
    a0 = to_middle(p0)
    cot_end_x = swap_x(cot_end)
    cot_end_s, cot_far_s = swap_core(cot_end), swap_core(cot_far)
    p1, p2 = partial_of(1, ids), partial_of(2, ids)

    p1, p0, a0, cot_far, r01, cot_end_x, ids = gated((p1, p0, a0, cot_far, r01, cot_end_x, ids), (cot_end_s, cot_far_s))
    a1 = to_middle(p1)
    s0 = both(p0, a0)
    o0 = across(s0)
    cot_far_x = swap_x(cot_far)
    y01 = swap_y(r01)
    cot_end_xs = swap_core(cot_end_x)
    p3 = partial_of(3, ids)

    p2, p1, a1, cot_far_x, cot_far_end = gated((p2, p1, a1, cot_far_x, cot_far_end), (cot_end_xs, y01))
    a2 = to_middle(p2)
    s1 = both(p1, a1)
    o1 = across(s1)
    cot_far_end_x = swap_x(cot_far_end)
    cot_far_xs, cot_far_end_s = swap_core(cot_far_x), swap_core(cot_far_end)

    f0 = mixed_of(0, s0, o0)
    p3, p2, a2, f0, cot_far_end_x = gated((p3, p2, a2, f0, cot_far_end_x), (cot_far_xs, cot_far_end_s))
    f0_x = swap_x(f0)
    a3 = to_middle(p3)
    s2 = both(p2, a2)
    o2 = across(s2)
    f0_s, cot_far_end_xs = swap_core(f0), swap_core(cot_far_end_x)

    f1 = mixed_of(1, s1, o1)
    f1, f0_x = gated((f1, f0_x), (f0_s, cot_far_end_xs))
    f1_x = swap_x(f1)
    p3, a3, own01 = gated((p3, a3, own01), ())
    e01 = to_middle(own01)
    s3 = both(p3, a3)
    o3 = across(s3)
    f1_s, f0_xs = swap_core(f1), swap_core(f0_x)

    f2 = mixed_of(2, s2, o2)
    f2, f1_x = gated((f2, f1_x), (f1_s, f0_xs))
    f2_x = swap_x(f2)
    e01, own23 = gated((e01, own23), ())
    e23 = to_middle(own23)
    e0, e1 = gated((e01[0], e01[1]), (o2,))
    r0 = across(e0)
    ye01 = swap_y(e01)
    f2_s, f1_xs = swap_core(f2), swap_core(f1_x)

    f3 = mixed_of(3, s3, o3)
    f3, f2_x = gated((f3, f2_x), (f2_s, f1_xs))
    f3_x = swap_x(f3)
    (e1,) = gated((e1,), (o3,))
    r1 = across(e1)
    f3_s, f2_xs = swap_core(f3), swap_core(f2_x)
    r0, ye01 = gated((r0, ye01), ())
    y0 = swap_y(r0)
    (h2,) = gated((jnp.stack([own23[0], e23[0]]),), (r0,))
    r2 = across(h2)

    f3_x, y0 = gated((f3_x, y0), (f3_s, f2_xs))
    f3_xs = swap_core(f3_x)
    r1, y0 = gated((r1, y0), ())
    y1 = swap_y(r1)
    (h3,) = gated((jnp.stack([own23[1], e23[1]]),), (r1,))
    r3 = across(h3)
    (e23,) = gated((e23,), (y0,))
    ye23 = swap_y(e23)
    features = [[f0, f0_s, f0_x, f0_xs], [f1, f1_s, f1_x, f1_xs], [f2, f2_s, f2_x, f2_xs], [f3, f3_s, f3_x, f3_xs]]
    cotangents = [
        [cot, cot_s, cot_x, cot_xs],
        [cot_end, cot_end_s, cot_end_x, cot_end_xs],
        [cot_far_end, cot_far_end_s, cot_far_end_x, cot_far_end_xs],
        [cot_far, cot_far_s, cot_far_x, cot_far_xs],
    ]
    scalars = jnp.stack([plane ^ column, part, plane]).astype(jnp.int32)
    bias = b_in.reshape(1, -1)

    def run(chunk, *moved):
        return hidden_chunk(chunk, scalars, features, cotangents, packs[chunk], *moved, bias)

    g0 = run(0, [(r01, 0), (r0, None), (e01, 0), (y01, 0), (y0, None), (ye01, 0)])

    r2, y1, end0 = gated((r2, y1, g0[2]), ())
    y2 = swap_y(r2)
    c0 = to_end(end0)
    g1 = run(1, [(r01, 1), (r1, None), (e01, 1), (y01, 1), (y1, None), (ye01, 1)])

    r3, y2, end1, c0 = gated((r3, y2, g1[2], c0), (ye23,))
    y3 = swap_y(r3)
    c1 = to_end(end1)
    g2 = run(2, [(r2, 0), (r2, 1), (e23, 0), (y2, 0), (y2, 1), (ye23, 0)])

    y3, end2, c1 = gated((y3, g2[2], c1), ())
    c2 = to_end(end2)
    g3 = run(3, [(r3, 0), (r3, 1), (e23, 1), (y3, 0), (y3, 1), (ye23, 1)])
    end3, c2 = gated((g3[2], c2), ())
    c3 = to_end(end3)

    is_middle = (plane == 1) | (plane == 2)
    grad_w_in = jnp.zeros((width, hidden_units), f32)
    grad_w_out = jnp.zeros((hidden_units, width), f32)
    biases = []
    for chunk, ((own_in, own_out, _, own_bias), end) in enumerate(zip((g0, g1, g2, g3), (c0, c1, c2, c3))):
        end = end.astype(f32)
        here = slice(chunk * size, (chunk + 1) * size)
        end_out = end[width : 2 * width].reshape(width // size, size, size).transpose(1, 0, 2).reshape(size, width)
        grad_w_in = grad_w_in.at[:, here].set(jnp.where(is_middle, own_in, end[:width]))
        grad_w_out = grad_w_out.at[here].set(jnp.where(is_middle, own_out, end_out))
        high, middle, low = (end[2 * width + i] for i in range(3))
        biases.append(jnp.where(is_middle, own_bias[0], (high + middle) + low))
    return (grad_w_in, grad_w_out, jnp.concatenate(biases))


def gathered(previous_embedding, tile_source, tile_mask, row_order, w_in, b_in, w_out, grad_out):
    groups = lax.axis_size("vocab")
    blocks, slots_per = tile_source.shape
    tiles_here = previous_embedding.shape[0] // TILE_SIZE
    columns = previous_embedding.shape[1]
    flat_source = tile_source.reshape(-1)
    owner_dev = flat_source // tiles_here
    local_tile = flat_source % tiles_here
    total_slots = flat_source.shape[0]
    capacity = max(2, 2 * total_slots // groups)
    slot_ids = jnp.arange(total_slots)
    earlier = slot_ids[None, :] < slot_ids[:, None]
    same_owner = owner_dev[None, :] == owner_dev[:, None]
    position = jnp.sum(jnp.where(earlier & same_owner, 1, 0), axis=1).astype(jnp.int32)
    owner_hit = owner_dev[:, None] == jnp.arange(groups)[None, :]
    place_hit = position[:, None] == jnp.arange(capacity)[None, :]
    placed = owner_hit[:, :, None] & place_hit[:, None, :]
    slot_index = owner_dev * capacity + position
    mask_values = tile_mask.astype(jnp.bfloat16)
    requests = jnp.sum(jnp.where(placed, local_tile[:, None, None], 0), axis=0)
    tile_lookup = previous_embedding.reshape(tiles_here, TILE_SIZE, columns)
    found_tiles = jnp.take(
        tile_lookup,
        lax.all_to_all(requests, "vocab", split_axis=0, concat_axis=0, tiled=True),
        axis=0,
    )
    arrived = lax.all_to_all(found_tiles, "vocab", split_axis=0, concat_axis=0, tiled=True)
    picked = arrived.reshape(groups * capacity, TILE_SIZE, columns)[slot_index]
    picked = picked.reshape(blocks, slots_per, TILE_SIZE, columns)
    summed = jnp.einsum("bkrc,bkcd->brd", mask_values, picked, preferred_element_type=jnp.float32)
    counts = jnp.sum(tile_mask, axis=(1, 3))
    inverse = 1.0 / jnp.maximum(counts, 1).astype(jnp.float32)
    mixed = (summed * inverse[:, :, None]).astype(jnp.bfloat16).reshape(blocks * TILE_SIZE, columns)
    rows_here = mixed.shape[0]
    ordered = mixed[row_order % rows_here]
    w_in_full = lax.all_gather(w_in, "vocab", axis=0, tiled=True)
    features = lax.all_gather(ordered, ("mp", "sub"), axis=1, tiled=True)
    preact = jnp.dot(features, w_in_full, preferred_element_type=jnp.float32) + b_in
    activation, act_slope = gelu_parts(preact)
    hidden = activation.astype(jnp.bfloat16)
    w_out_full = lax.all_gather(w_out, "vocab", axis=1, tiled=True)
    cotangent = lax.all_gather(grad_out, ("mp", "sub"), axis=1, tiled=True)
    hidden_grad = lax.dot_general(
        cotangent, w_out_full, (((1,), (1,)), ((), ())), preferred_element_type=jnp.float32
    )
    pre_grad = (hidden_grad * act_slope).astype(jnp.bfloat16)
    grad_bias = lax.psum(jnp.sum(pre_grad.astype(jnp.float32), axis=0), "vocab")
    grad_w_in = lax.psum_scatter(
        lax.dot_general(
            features, pre_grad, (((0,), (0,)), ((), ())), preferred_element_type=jnp.float32
        ).astype(jnp.bfloat16),
        "vocab",
        scatter_dimension=0,
        tiled=True,
    ).astype(jnp.float32)
    grad_w_out = (
        lax.psum_scatter(
            lax.dot_general(
                cotangent, hidden, (((0,), (0,)), ((), ())), preferred_element_type=jnp.float32
            ).astype(jnp.bfloat16),
            "vocab",
            scatter_dimension=0,
            tiled=True,
        )
        .astype(jnp.float32)
        .T
    )
    return (grad_w_in, grad_w_out, grad_bias)


def solution(mesh):
    placed = (
        P("vocab", ("mp", "sub")),
        P(("groups", "vocab"), None),
        P(("groups", "vocab"), None, None, None),
        P(("groups", "vocab")),
        P("vocab", ("mp", "sub")),
        P(("mp", "sub")),
        P(("mp", "sub"), "vocab"),
        P(("groups", "vocab"), ("mp", "sub")),
    )
    return jax.shard_map(
        middle_planes if planes_fit(mesh) else gathered,
        mesh=mesh,
        in_specs=placed,
        out_specs=(
            P(("groups", "vocab"), ("mp", "sub")),
            P(("groups", "mp", "sub"), "vocab"),
            P(("groups", "mp", "sub")),
        ),
        check_vma=False,
    )
```

```python
import functools

import jax
import jax.numpy as jnp
from jax import lax
from jax.experimental import pallas as pl
from jax.experimental.pallas import tpu as pltpu
from jax.sharding import PartitionSpec as P

TILE_SIZE = 128


tanh_scale = 0.7978845608028654
cubic_term = 0.044715


def gelu_parts(values):
    inner_arg = tanh_scale * (values + cubic_term * values * values * values)
    tangent = jnp.tanh(inner_arg)
    activation = 0.5 * values * (1.0 + tangent)
    act_slope = 0.5 * (1.0 + tangent) + 0.5 * values * (1.0 - tangent * tangent) * tanh_scale * (
        1.0 + 3.0 * cubic_term * values * values
    )
    return (activation, act_slope)


TO_MIDDLE = [(0, 1), (3, 2)]
ACROSS = [(1, 2), (2, 1)]
TO_END = [(1, 0), (2, 3)]
SWAP = [(0, 1), (1, 0)]

ROW_TILE = 512
AHEAD = 1
HIDDEN_CHUNK = 256
HEADER_ROWS = 16
BIAS_ROWS = 16
VMEM_BYTES = 60 * 1024 * 1024


def planes_fit(mesh):
    return dict(mesh.shape) == dict(groups=2, vocab=4, mp=2, sub=2)


def gated(values, results):
    return lax.optimization_barrier((tuple(values), tuple(results)))[0]


def mix_kernel(group, places, tile_ids, block_ids, *refs):
    tiles, (own_masks, sibling_masks, out, total) = refs[:places], refs[places:]
    total[...] = jnp.zeros_like(total)
    half = places // 2
    for place in range(places):
        masks = own_masks if place < half else sibling_masks
        mask = masks[0, (place % half) * TILE_SIZE : (place % half + 1) * TILE_SIZE, :]
        start = pl.multiple_of(block_ids[group * places + place] * TILE_SIZE, TILE_SIZE)
        total[pl.ds(start, TILE_SIZE), :] += jnp.dot(mask, tiles[place][0], preferred_element_type=jnp.float32)
    out[...] = total[...].astype(out.dtype)


def mix_group(group, rows, places, tile_ids, block_ids, tile_lookup, own_masks, sibling_masks):
    columns = tile_lookup.shape[2]

    def tile_spec(place):
        return pl.BlockSpec((1, TILE_SIZE, columns), lambda i, ids, blocks: (ids[group * places + place], 0, 0))

    mask_spec = pl.BlockSpec((1,) + own_masks.shape[1:], lambda i, ids, blocks: (group, 0, 0))
    return pl.pallas_call(
        functools.partial(mix_kernel, group, places),
        out_shape=jax.ShapeDtypeStruct((rows, columns), jnp.bfloat16),
        grid_spec=pltpu.PrefetchScalarGridSpec(
            num_scalar_prefetch=2,
            grid=(1,),
            in_specs=[tile_spec(place) for place in range(places)] + [mask_spec] * 2,
            out_specs=pl.BlockSpec((rows, columns), lambda i, ids, blocks: (0, 0)),
            scratch_shapes=[pltpu.VMEM((rows, columns), jnp.float32)],
        ),
        compiler_params=pltpu.CompilerParams(vmem_limit_bytes=VMEM_BYTES),
        cost_estimate=pl.CostEstimate(
            flops=2 * places * TILE_SIZE * TILE_SIZE * columns,
            bytes_accessed=2 * places * TILE_SIZE * columns + 2 * rows * columns,
            transcendentals=0,
        ),
        name=f"mix_group_{group}",
    )(tile_ids, block_ids, *([tile_lookup] * places), own_masks, sibling_masks)


def chunk_kernel(pieces, far_places, scalars, *refs):
    feature_refs = [refs[g * pieces : (g + 1) * pieces] for g in range(4)]
    cotangent_refs = [refs[(4 + g) * pieces : (5 + g) * pieces] for g in range(4)]
    (own_pack, *fars, bias, grad_in, grad_out, end_grads, grad_bias,
     features, cotangent, in_all, out_all, sum_in, sum_out, sum_bias, sems, weight_sems) = refs[8 * pieces :]
    fars = [far if place is None else far.at[place] for far, place in zip(fars, far_places)]
    own, part, plane = scalars[0], scalars[1], scalars[2]
    size = in_all.shape[1]
    rows, width = feature_refs[0][0].shape
    tiles = rows // ROW_TILE

    def weights(source, target, k, kind):
        target = target.at[pl.ds(pl.multiple_of((own ^ k) * width, width), width)]
        return pltpu.make_async_copy(source, target, weight_sems.at[kind, k])

    for kind, target in ((0, in_all), (1, out_all)):
        weights(own_pack.at[pl.ds(kind * width, width)], target, 0, kind).start()
    for half in range(2):

        @pl.when(part == half)
        def _():
            for i, k in ((0, 3), (1, 2), (2, 1)):
                weights(fars[3 * half + i], in_all, k, 0).start()
                weights(fars[3 - 3 * half + i], out_all, k, 1).start()

    def move(source, target, kind, step, tile, k):
        from_rows = pl.ds(pl.multiple_of(tile * ROW_TILE, ROW_TILE), ROW_TILE)
        to_rows = pl.ds(pl.multiple_of(step * ROW_TILE, ROW_TILE), ROW_TILE)
        return pltpu.make_async_copy(
            source.at[from_rows], target.at[to_rows, pl.ds(k * width, width)], sems.at[kind, step, k]
        )

    def fetch(step):
        group, tile = step // tiles, step % tiles
        for i in range(4):

            @pl.when(group == i)
            def _():
                for k in range(pieces):
                    move(feature_refs[i][k], features, 0, step, tile, k).start()

            @pl.when((plane ^ group) == i)
            def _():
                for k in range(pieces):
                    move(cotangent_refs[i][k], cotangent, 1, step, tile, k).start()

    for step in range(AHEAD):
        fetch(step)
    sum_in[...] = jnp.zeros_like(sum_in)
    sum_out[...] = jnp.zeros_like(sum_out)
    sum_bias[...] = jnp.zeros_like(sum_bias)
    for k in range(pieces):
        weights(fars[0], in_all, k, 0).wait()
        weights(fars[0], out_all, k, 1).wait()

    @pl.loop(0, 4 * tiles)
    def _(step):
        @pl.when(step + AHEAD < 4 * tiles)
        def _():
            fetch(step + AHEAD)

        here = pl.ds(pl.multiple_of(step * ROW_TILE, ROW_TILE), ROW_TILE)
        for k in range(pieces):
            move(feature_refs[0][k], features, 0, step, 0, k).wait()
            move(cotangent_refs[0][k], cotangent, 1, step, 0, k).wait()
        preact = bias[...] + jnp.dot(features[here, :], in_all[...], preferred_element_type=jnp.float32)
        hidden_grad = jnp.dot(cotangent[here, :], out_all[...], preferred_element_type=jnp.float32)
        activation, act_slope = gelu_parts(preact)
        hidden = activation.astype(jnp.bfloat16)
        pre_grad = (hidden_grad * act_slope).astype(jnp.bfloat16)
        sum_bias[...] += jnp.sum(pre_grad.astype(jnp.float32), axis=0, keepdims=True)
        hidden, pre_grad = hidden.T, pre_grad.T
        for j in range(2):
            columns = pl.ds(pl.multiple_of((own ^ j) * width, width), width)
            sum_in[j] += jnp.dot(pre_grad, features[here, columns], preferred_element_type=jnp.float32)
            sum_out[j] += jnp.dot(hidden, cotangent[here, columns], preferred_element_type=jnp.float32)

    grad_in[...] = sum_in[0].T
    grad_out[...] = sum_out[0]
    end_grads[:width, :] = sum_in[1].T.astype(jnp.bfloat16)
    for q in range(width // size):
        end_grads[width + q * size : width + (q + 1) * size, :] = sum_out[1, :, q * size : (q + 1) * size].astype(jnp.bfloat16)
    grad_bias[...] = sum_bias[...]
    part_rows = lax.broadcasted_iota(jnp.int32, (BIAS_ROWS, size), 0)
    rest = sum_bias[...]
    parts = jnp.zeros((BIAS_ROWS, size), jnp.float32)
    for i in range(3):
        rounded = rest.astype(jnp.bfloat16).astype(jnp.float32)
        parts = jnp.where(part_rows == i, rounded, parts)
        rest = rest - rounded
    end_grads[2 * width :, :] = parts.astype(jnp.bfloat16)


def hidden_chunk(chunk, scalars, features, cotangents, own_pack, fars, bias):
    groups, pieces = len(features), len(features[0])
    rows, width = features[0][0].shape
    size = HIDDEN_CHUNK
    flat = [piece for group in features for piece in group] + [piece for group in cotangents for piece in group]
    flat += [own_pack] + [array for array, _ in fars]

    def whole(array):
        return pl.BlockSpec(array.shape, lambda i, s: (0,) * array.ndim)

    shapes = [
        jax.ShapeDtypeStruct((width, size), jnp.float32),
        jax.ShapeDtypeStruct((size, width), jnp.float32),
        jax.ShapeDtypeStruct((2 * width + BIAS_ROWS, size), jnp.bfloat16),
        jax.ShapeDtypeStruct((1, size), jnp.float32),
    ]
    return pl.pallas_call(
        functools.partial(chunk_kernel, pieces, [place for _, place in fars]),
        out_shape=shapes,
        grid_spec=pltpu.PrefetchScalarGridSpec(
            num_scalar_prefetch=1,
            grid=(1,),
            in_specs=[pl.BlockSpec(memory_space=pl.ANY)] * len(flat) + [pl.BlockSpec((1, size), lambda i, s: (0, chunk))],
            out_specs=[whole(shape) for shape in shapes],
            scratch_shapes=[
                pltpu.VMEM((groups * rows, pieces * width), jnp.bfloat16),
                pltpu.VMEM((groups * rows, pieces * width), jnp.bfloat16),
                pltpu.VMEM((pieces * width, size), jnp.bfloat16),
                pltpu.VMEM((pieces * width, size), jnp.bfloat16),
                pltpu.VMEM((2, size, width), jnp.float32),
                pltpu.VMEM((2, size, width), jnp.float32),
                pltpu.VMEM((1, size), jnp.float32),
                pltpu.SemaphoreType.DMA((2, groups * rows // ROW_TILE, pieces)),
                pltpu.SemaphoreType.DMA((2, pieces)),
            ],
        ),
        compiler_params=pltpu.CompilerParams(vmem_limit_bytes=VMEM_BYTES),
        cost_estimate=pl.CostEstimate(
            flops=2 * 2 * groups * rows * (pieces + 2) * width * size,
            bytes_accessed=2 * 2 * groups * pieces * rows * width,
            transcendentals=groups * rows * size,
        ),
        name=f"hidden_chunk_{chunk}",
    )(scalars, *flat, bias)


def pack_kernel(half, blocks, slot_of, filled, masks, numbers, sent):
    slots_per = masks.shape[0] // blocks
    planes = sent.shape[0]

    @pl.loop(0, planes * half)
    def _(place):
        row = pl.multiple_of(lax.rem(place, half) * TILE_SIZE, TILE_SIZE)
        sent[place // half, pl.ds(row, TILE_SIZE), :] = (masks[slot_of[place]] * filled[place]).astype(sent.dtype)

    row_ids = lax.broadcasted_iota(jnp.int32, (HEADER_ROWS, TILE_SIZE), 0)
    ones = jnp.ones((HEADER_ROWS, TILE_SIZE), jnp.bfloat16)
    header = jnp.zeros((HEADER_ROWS, TILE_SIZE), jnp.float32)
    for block in range(blocks):
        total = masks[block * slots_per]
        for slot in range(1, slots_per):
            total += masks[block * slots_per + slot]
        counts = lax.dot_general(
            ones, total.astype(jnp.bfloat16), (((1,), (1,)), ((), ())), preferred_element_type=jnp.float32
        ).astype(jnp.int32)
        header = jnp.where(row_ids == 1 + block, (counts // TILE_SIZE).astype(jnp.float32), header)
        header = jnp.where(row_ids == 1 + blocks + block, (counts % TILE_SIZE).astype(jnp.float32), header)
    for plane in range(planes):
        own_numbers = numbers[plane : plane + 1, :].astype(jnp.float32)
        sent[plane, half * TILE_SIZE :, :] = jnp.where(row_ids == 0, own_numbers, header).astype(sent.dtype)


def pack_masks(slot_of, filled, masks, numbers, blocks):
    planes, half = slot_of.shape
    shape = jax.ShapeDtypeStruct((planes, half * TILE_SIZE + HEADER_ROWS, TILE_SIZE), jnp.bfloat16)
    return pl.pallas_call(
        functools.partial(pack_kernel, half, blocks),
        out_shape=shape,
        grid_spec=pltpu.PrefetchScalarGridSpec(
            num_scalar_prefetch=2,
            grid=(1,),
            in_specs=[
                pl.BlockSpec(masks.shape, lambda i, s, f: (0, 0, 0)),
                pl.BlockSpec(numbers.shape, lambda i, s, f: (0, 0)),
            ],
            out_specs=pl.BlockSpec(shape.shape, lambda i, s, f: (0, 0, 0)),
        ),
        compiler_params=pltpu.CompilerParams(vmem_limit_bytes=VMEM_BYTES),
        name="pack_masks",
    )(slot_of.reshape(-1), filled.astype(jnp.int32).reshape(-1), masks, numbers)


def middle_planes(previous_embedding, tile_source, tile_mask, row_order, w_in, b_in, w_out, grad_out):
    plane, part, core = lax.axis_index("vocab"), lax.axis_index("groups"), lax.axis_index("sub")
    column = 2 * lax.axis_index("mp") + core
    planes = lax.axis_size("vocab")
    blocks, slots_per = tile_source.shape
    total_slots = blocks * slots_per
    tiles_here = previous_embedding.shape[0] // TILE_SIZE
    columns = previous_embedding.shape[1]
    tile_lookup = previous_embedding.reshape(tiles_here, TILE_SIZE, columns)
    rows = row_order.shape[0]
    places = 2 * total_slots // planes
    half = places // 2
    bf16, f32 = jnp.bfloat16, jnp.float32

    def to_middle(array):
        return lax.ppermute(array, "vocab", TO_MIDDLE)

    def across(array):
        return lax.ppermute(array, "vocab", ACROSS)

    def to_end(array):
        return lax.ppermute(array, "vocab", TO_END)

    def swap_x(array):
        return lax.ppermute(array, "mp", SWAP)

    def swap_y(array):
        return lax.ppermute(array, "groups", SWAP)

    def swap_core(array):
        return lax.ppermute(array, "sub", SWAP)

    source = tile_source.reshape(-1)
    owner = source // tiles_here
    slot_ids = jnp.arange(total_slots)
    earlier = slot_ids[None, :] < slot_ids[:, None]
    position = jnp.sum(jnp.where(earlier & (owner[None, :] == owner[:, None]), 1, 0), axis=1)
    my_places = core * half + jnp.arange(half)
    hit = (owner[:, None, None] == jnp.arange(planes)[None, :, None]) & (
        position[:, None, None] == my_places[None, None, :]
    )
    slot_of = jnp.sum(jnp.where(hit, slot_ids[:, None, None], 0), axis=0)
    filled = jnp.any(hit, axis=0)
    numbers = jnp.concatenate(
        [
            jnp.sum(jnp.where(hit, (source % tiles_here)[:, None, None], 0), axis=0),
            jnp.sum(jnp.where(hit, (slot_ids // slots_per)[:, None, None], 0), axis=0),
        ],
        axis=1,
    )
    numbers = jnp.pad(numbers, ((0, 0), (0, TILE_SIZE - 2 * half)))
    masks = tile_mask.reshape(total_slots, TILE_SIZE, TILE_SIZE)
    sent = pack_masks(slot_of, filled, masks, numbers, blocks)

    placed = (row_order % rows)[None, :] == jnp.arange(rows)[:, None]
    cot = jnp.dot(placed.astype(bf16), grad_out, preferred_element_type=f32).astype(bf16)

    hidden_units, width = w_out.shape
    size = HIDDEN_CHUNK
    chunks = hidden_units // size
    packs = []
    for chunk in range(chunks):
        here = slice(chunk * size, (chunk + 1) * size)
        packs.append(jnp.concatenate([w_in[:, here], w_out[here].T], axis=0))

    def my_half(pack):
        return lax.dynamic_slice_in_dim(pack, part * width, width, axis=0)

    def both(a, b):
        return (a.astype(f32) + b.astype(f32)).astype(bf16)

    def mixed_of(group, side, other):
        return ((side.astype(f32) + other.astype(f32)) * all_inverse[group][:, None]).astype(bf16)

    def partial_of(group, ids):
        return mix_group(group, rows, places, ids, block_ids, tile_lookup, masks, sibling)

    def numbers_of(array):
        header = array[:, half * TILE_SIZE, : 2 * half].astype(jnp.int32)
        return header[:, :half], header[:, half:]

    own01 = jnp.stack([my_half(packs[0]), my_half(packs[1])])
    own23 = jnp.stack([my_half(packs[2]), my_half(packs[3])])
    got = lax.all_to_all(sent, "vocab", split_axis=0, concat_axis=0, tiled=True)
    cot_x = swap_x(cot)

    masks, cot, cot_x, own01, own23 = gated((got, cot, cot_x, own01, own23), ())
    sibling = swap_core(masks)
    cot_far = across(cot)
    r01 = across(own01)
    cot_end = to_middle(cot)
    cot_s, cot_xs = swap_core(cot), swap_core(cot_x)
    own_numbers, sibling_numbers = numbers_of(masks), numbers_of(sibling)
    tile_ids, block_ids = (jnp.concatenate(pair, axis=1).reshape(-1) for pair in zip(own_numbers, sibling_numbers))
    first = half * TILE_SIZE + 1
    count_high, count_low = (masks[:, first + i * blocks : first + (i + 1) * blocks].astype(f32) for i in range(2))
    all_inverse = (1.0 / jnp.maximum(count_high * TILE_SIZE + count_low, 1.0)).reshape(planes, rows)
    p0 = partial_of(0, tile_ids)

    p0, cot_end, cot_far, ids = gated((p0, cot_end, cot_far, tile_ids), (cot_s, cot_xs, all_inverse))
    cot_far_end = across(cot_end)
    a0 = to_middle(p0)
    cot_end_x = swap_x(cot_end)
    cot_end_s, cot_far_s = swap_core(cot_end), swap_core(cot_far)
    p1, p2 = partial_of(1, ids), partial_of(2, ids)

    p1, p0, a0, cot_far, r01, cot_end_x, ids = gated((p1, p0, a0, cot_far, r01, cot_end_x, ids), (cot_end_s, cot_far_s))
    a1 = to_middle(p1)
    s0 = both(p0, a0)
    o0 = across(s0)
    cot_far_x = swap_x(cot_far)
    y01 = swap_y(r01)
    cot_end_xs = swap_core(cot_end_x)
    p3 = partial_of(3, ids)

    p2, p1, a1, cot_far_x, cot_far_end = gated((p2, p1, a1, cot_far_x, cot_far_end), (cot_end_xs, y01))
    a2 = to_middle(p2)
    s1 = both(p1, a1)
    o1 = across(s1)
    cot_far_end_x = swap_x(cot_far_end)
    cot_far_xs, cot_far_end_s = swap_core(cot_far_x), swap_core(cot_far_end)

    f0 = mixed_of(0, s0, o0)
    p3, p2, a2, f0, cot_far_end_x = gated((p3, p2, a2, f0, cot_far_end_x), (cot_far_xs, cot_far_end_s))
    f0_x = swap_x(f0)
    a3 = to_middle(p3)
    s2 = both(p2, a2)
    o2 = across(s2)
    f0_s, cot_far_end_xs = swap_core(f0), swap_core(cot_far_end_x)

    f1 = mixed_of(1, s1, o1)
    f1, f0_x = gated((f1, f0_x), (f0_s, cot_far_end_xs))
    f1_x = swap_x(f1)
    p3, a3, own01 = gated((p3, a3, own01), ())
    e01 = to_middle(own01)
    s3 = both(p3, a3)
    o3 = across(s3)
    f1_s, f0_xs = swap_core(f1), swap_core(f0_x)

    f2 = mixed_of(2, s2, o2)
    f2, f1_x = gated((f2, f1_x), (f1_s, f0_xs))
    f2_x = swap_x(f2)
    e01, o2 = gated((e01, o2), ())
    r_e01 = across(e01)
    ye01 = swap_y(e01)
    f2_s, f1_xs = swap_core(f2), swap_core(f1_x)

    f3 = mixed_of(3, s3, o3)
    f3, f2_x, own23 = gated((f3, f2_x, own23), (f2_s, f1_xs, ye01))
    f3_x = swap_x(f3)
    e23 = to_middle(own23)
    f3_s, f2_xs = swap_core(f3), swap_core(f2_x)
    r_e01, f3_s = gated((r_e01, f3_s), (f2_xs,))
    y_e01 = swap_y(r_e01)

    f3_x, y_e01 = gated((f3_x, y_e01), (f3_s,))
    f3_xs = swap_core(f3_x)
    r2 = across(jnp.stack([own23[0], e23[0]]))
    r3 = across(jnp.stack([own23[1], e23[1]]))
    ye23 = swap_y(e23)
    features = [[f0, f0_s, f0_x, f0_xs], [f1, f1_s, f1_x, f1_xs], [f2, f2_s, f2_x, f2_xs], [f3, f3_s, f3_x, f3_xs]]
    cotangents = [
        [cot, cot_s, cot_x, cot_xs],
        [cot_end, cot_end_s, cot_end_x, cot_end_xs],
        [cot_far_end, cot_far_end_s, cot_far_end_x, cot_far_end_xs],
        [cot_far, cot_far_s, cot_far_x, cot_far_xs],
    ]
    scalars = jnp.stack([plane ^ column, part, plane]).astype(jnp.int32)
    bias = b_in.reshape(1, -1)

    def run(chunk, *moved):
        return hidden_chunk(chunk, scalars, features, cotangents, packs[chunk], *moved, bias)

    g0 = run(0, [(r01, 0), (r_e01, 0), (e01, 0), (y01, 0), (y_e01, 0), (ye01, 0)])

    r2, end0 = gated((r2, g0[2]), ())
    y2 = swap_y(r2)
    c0 = to_end(end0)
    g1 = run(1, [(r01, 1), (r_e01, 1), (e01, 1), (y01, 1), (y_e01, 1), (ye01, 1)])

    r3, y2, end1, c0 = gated((r3, y2, g1[2], c0), (ye23,))
    y3 = swap_y(r3)
    c1 = to_end(end1)
    g2 = run(2, [(r2, 0), (r2, 1), (e23, 0), (y2, 0), (y2, 1), (ye23, 0)])

    y3, end2, c1 = gated((y3, g2[2], c1), ())
    c2 = to_end(end2)
    g3 = run(3, [(r3, 0), (r3, 1), (e23, 1), (y3, 0), (y3, 1), (ye23, 1)])
    end3, c0, c1, c2 = gated((g3[2], c0, c1, c2), ())
    c3 = to_end(end3)

    is_middle = (plane == 1) | (plane == 2)
    grad_w_in = jnp.zeros((width, hidden_units), f32)
    grad_w_out = jnp.zeros((hidden_units, width), f32)
    biases = []
    for chunk, ((own_in, own_out, _, own_bias), end) in enumerate(zip((g0, g1, g2, g3), (c0, c1, c2, c3))):
        end = end.astype(f32)
        here = slice(chunk * size, (chunk + 1) * size)
        end_out = end[width : 2 * width].reshape(width // size, size, size).transpose(1, 0, 2).reshape(size, width)
        grad_w_in = grad_w_in.at[:, here].set(jnp.where(is_middle, own_in, end[:width]))
        grad_w_out = grad_w_out.at[here].set(jnp.where(is_middle, own_out, end_out))
        high, middle, low = (end[2 * width + i] for i in range(3))
        biases.append(jnp.where(is_middle, own_bias[0], (high + middle) + low))
    return (grad_w_in, grad_w_out, jnp.concatenate(biases))


def gathered(previous_embedding, tile_source, tile_mask, row_order, w_in, b_in, w_out, grad_out):
    groups = lax.axis_size("vocab")
    blocks, slots_per = tile_source.shape
    tiles_here = previous_embedding.shape[0] // TILE_SIZE
    columns = previous_embedding.shape[1]
    flat_source = tile_source.reshape(-1)
    owner_dev = flat_source // tiles_here
    local_tile = flat_source % tiles_here
    total_slots = flat_source.shape[0]
    capacity = max(2, 2 * total_slots // groups)
    slot_ids = jnp.arange(total_slots)
    earlier = slot_ids[None, :] < slot_ids[:, None]
    same_owner = owner_dev[None, :] == owner_dev[:, None]
    position = jnp.sum(jnp.where(earlier & same_owner, 1, 0), axis=1).astype(jnp.int32)
    owner_hit = owner_dev[:, None] == jnp.arange(groups)[None, :]
    place_hit = position[:, None] == jnp.arange(capacity)[None, :]
    placed = owner_hit[:, :, None] & place_hit[:, None, :]
    slot_index = owner_dev * capacity + position
    mask_values = tile_mask.astype(jnp.bfloat16)
    requests = jnp.sum(jnp.where(placed, local_tile[:, None, None], 0), axis=0)
    tile_lookup = previous_embedding.reshape(tiles_here, TILE_SIZE, columns)
    found_tiles = jnp.take(
        tile_lookup,
        lax.all_to_all(requests, "vocab", split_axis=0, concat_axis=0, tiled=True),
        axis=0,
    )
    arrived = lax.all_to_all(found_tiles, "vocab", split_axis=0, concat_axis=0, tiled=True)
    picked = arrived.reshape(groups * capacity, TILE_SIZE, columns)[slot_index]
    picked = picked.reshape(blocks, slots_per, TILE_SIZE, columns)
    summed = jnp.einsum("bkrc,bkcd->brd", mask_values, picked, preferred_element_type=jnp.float32)
    counts = jnp.sum(tile_mask, axis=(1, 3))
    inverse = 1.0 / jnp.maximum(counts, 1).astype(jnp.float32)
    mixed = (summed * inverse[:, :, None]).astype(jnp.bfloat16).reshape(blocks * TILE_SIZE, columns)
    rows_here = mixed.shape[0]
    ordered = mixed[row_order % rows_here]
    w_in_full = lax.all_gather(w_in, "vocab", axis=0, tiled=True)
    features = lax.all_gather(ordered, ("mp", "sub"), axis=1, tiled=True)
    preact = jnp.dot(features, w_in_full, preferred_element_type=jnp.float32) + b_in
    activation, act_slope = gelu_parts(preact)
    hidden = activation.astype(jnp.bfloat16)
    w_out_full = lax.all_gather(w_out, "vocab", axis=1, tiled=True)
    cotangent = lax.all_gather(grad_out, ("mp", "sub"), axis=1, tiled=True)
    hidden_grad = lax.dot_general(
        cotangent, w_out_full, (((1,), (1,)), ((), ())), preferred_element_type=jnp.float32
    )
    pre_grad = (hidden_grad * act_slope).astype(jnp.bfloat16)
    grad_bias = lax.psum(jnp.sum(pre_grad.astype(jnp.float32), axis=0), "vocab")
    grad_w_in = lax.psum_scatter(
        lax.dot_general(
            features, pre_grad, (((0,), (0,)), ((), ())), preferred_element_type=jnp.float32
        ).astype(jnp.bfloat16),
        "vocab",
        scatter_dimension=0,
        tiled=True,
    ).astype(jnp.float32)
    grad_w_out = (
        lax.psum_scatter(
            lax.dot_general(
                cotangent, hidden, (((0,), (0,)), ((), ())), preferred_element_type=jnp.float32
            ).astype(jnp.bfloat16),
            "vocab",
            scatter_dimension=0,
            tiled=True,
        )
        .astype(jnp.float32)
        .T
    )
    return (grad_w_in, grad_w_out, grad_bias)


def solution(mesh):
    placed = (
        P("vocab", ("mp", "sub")),
        P(("groups", "vocab"), None),
        P(("groups", "vocab"), None, None, None),
        P(("groups", "vocab")),
        P("vocab", ("mp", "sub")),
        P(("mp", "sub")),
        P(("mp", "sub"), "vocab"),
        P(("groups", "vocab"), ("mp", "sub")),
    )
    return jax.shard_map(
        middle_planes if planes_fit(mesh) else gathered,
        mesh=mesh,
        in_specs=placed,
        out_specs=(
            P(("groups", "vocab"), ("mp", "sub")),
            P(("groups", "mp", "sub"), "vocab"),
            P(("groups", "mp", "sub")),
        ),
        check_vma=False,
    )
```

```python
import functools

import jax
import jax.numpy as jnp
from jax import lax
from jax.experimental import pallas as pl
from jax.experimental.pallas import tpu as pltpu
from jax.sharding import PartitionSpec as P

TILE_SIZE = 128


tanh_scale = 0.7978845608028654
cubic_term = 0.044715


def gelu_parts(values):
    inner_arg = tanh_scale * (values + cubic_term * values * values * values)
    tangent = jnp.tanh(inner_arg)
    activation = 0.5 * values * (1.0 + tangent)
    act_slope = 0.5 * (1.0 + tangent) + 0.5 * values * (1.0 - tangent * tangent) * tanh_scale * (
        1.0 + 3.0 * cubic_term * values * values
    )
    return (activation, act_slope)


TO_MIDDLE = [(0, 1), (3, 2)]
ACROSS = [(1, 2), (2, 1)]
TO_END = [(1, 0), (2, 3)]
SWAP = [(0, 1), (1, 0)]

ROW_TILE = 512
AHEAD = 1
HIDDEN_CHUNK = 256
HEADER_ROWS = 16
BIAS_ROWS = 16
VMEM_BYTES = 60 * 1024 * 1024


def planes_fit(mesh):
    return dict(mesh.shape) == dict(groups=2, vocab=4, mp=2, sub=2)


def gated(values, results):
    return lax.optimization_barrier((tuple(values), tuple(results)))[0]


def mix_kernel(group, places, tile_ids, block_ids, *refs):
    tiles, (own_masks, sibling_masks, out, total) = refs[:places], refs[places:]
    total[...] = jnp.zeros_like(total)
    half = places // 2
    for place in range(places):
        masks = own_masks if place < half else sibling_masks
        mask = masks[0, (place % half) * TILE_SIZE : (place % half + 1) * TILE_SIZE, :]
        start = pl.multiple_of(block_ids[group * places + place] * TILE_SIZE, TILE_SIZE)
        total[pl.ds(start, TILE_SIZE), :] += jnp.dot(mask, tiles[place][0], preferred_element_type=jnp.float32)
    out[...] = total[...].astype(out.dtype)


def mix_group(group, rows, places, tile_ids, block_ids, tile_lookup, own_masks, sibling_masks):
    columns = tile_lookup.shape[2]

    def tile_spec(place):
        return pl.BlockSpec((1, TILE_SIZE, columns), lambda i, ids, blocks: (ids[group * places + place], 0, 0))

    mask_spec = pl.BlockSpec((1,) + own_masks.shape[1:], lambda i, ids, blocks: (group, 0, 0))
    return pl.pallas_call(
        functools.partial(mix_kernel, group, places),
        out_shape=jax.ShapeDtypeStruct((rows, columns), jnp.bfloat16),
        grid_spec=pltpu.PrefetchScalarGridSpec(
            num_scalar_prefetch=2,
            grid=(1,),
            in_specs=[tile_spec(place) for place in range(places)] + [mask_spec] * 2,
            out_specs=pl.BlockSpec((rows, columns), lambda i, ids, blocks: (0, 0)),
            scratch_shapes=[pltpu.VMEM((rows, columns), jnp.float32)],
        ),
        compiler_params=pltpu.CompilerParams(vmem_limit_bytes=VMEM_BYTES),
        cost_estimate=pl.CostEstimate(
            flops=2 * places * TILE_SIZE * TILE_SIZE * columns,
            bytes_accessed=2 * places * TILE_SIZE * columns + 2 * rows * columns,
            transcendentals=0,
        ),
        name=f"mix_group_{group}",
    )(tile_ids, block_ids, *([tile_lookup] * places), own_masks, sibling_masks)


def chunk_kernel(chunk, pieces, far_places, scalars, *refs):
    feature_refs = [refs[g * pieces : (g + 1) * pieces] for g in range(4)]
    cotangent_refs = [refs[(4 + g) * pieces : (5 + g) * pieces] for g in range(4)]
    (own_in, own_out, *fars, bias, grad_in, grad_out, end_grads, grad_bias,
     features, cotangent, in_all, out_all, sum_in, sum_out, sum_bias, sems, weight_sems) = refs[8 * pieces :]
    fars = [far if place is None else far.at[place] for far, place in zip(fars, far_places)]
    own, part, plane = scalars[0], scalars[1], scalars[2]
    size = in_all.shape[1]
    rows, width = feature_refs[0][0].shape
    tiles = rows // ROW_TILE

    def weights(source, target, k, kind):
        target = target.at[pl.ds(pl.multiple_of((own ^ k) * width, width), width)]
        return pltpu.make_async_copy(source, target, weight_sems.at[kind, k])

    for kind, (source, target) in enumerate(((own_in, in_all), (own_out, out_all))):
        weights(source.at[:, pl.ds(chunk * size, size)], target, 0, kind).start()
    for half in range(2):

        @pl.when(part == half)
        def _():
            for i, k in ((0, 3), (1, 2), (2, 1)):
                weights(fars[3 * half + i], in_all, k, 0).start()
                weights(fars[3 - 3 * half + i], out_all, k, 1).start()

    def move(source, target, kind, step, tile, k):
        from_rows = pl.ds(pl.multiple_of(tile * ROW_TILE, ROW_TILE), ROW_TILE)
        to_rows = pl.ds(pl.multiple_of(step * ROW_TILE, ROW_TILE), ROW_TILE)
        return pltpu.make_async_copy(
            source.at[from_rows], target.at[to_rows, pl.ds(k * width, width)], sems.at[kind, step, k]
        )

    def fetch(step):
        group, tile = step // tiles, step % tiles
        for i in range(4):

            @pl.when(group == i)
            def _():
                for k in range(pieces):
                    move(feature_refs[i][k], features, 0, step, tile, k).start()

            @pl.when((plane ^ group) == i)
            def _():
                for k in range(pieces):
                    move(cotangent_refs[i][k], cotangent, 1, step, tile, k).start()

    for step in range(AHEAD):
        fetch(step)
    sum_in[...] = jnp.zeros_like(sum_in)
    sum_out[...] = jnp.zeros_like(sum_out)
    sum_bias[...] = jnp.zeros_like(sum_bias)
    for k in range(pieces):
        weights(fars[0], in_all, k, 0).wait()
        weights(fars[0], out_all, k, 1).wait()

    @pl.loop(0, 4 * tiles)
    def _(step):
        @pl.when(step + AHEAD < 4 * tiles)
        def _():
            fetch(step + AHEAD)

        here = pl.ds(pl.multiple_of(step * ROW_TILE, ROW_TILE), ROW_TILE)
        for k in range(pieces):
            move(feature_refs[0][k], features, 0, step, 0, k).wait()
            move(cotangent_refs[0][k], cotangent, 1, step, 0, k).wait()
        preact = bias[...] + jnp.dot(features[here, :], in_all[...], preferred_element_type=jnp.float32)
        hidden_grad = jnp.dot(cotangent[here, :], out_all[...], preferred_element_type=jnp.float32)
        activation, act_slope = gelu_parts(preact)
        hidden = activation.astype(jnp.bfloat16)
        pre_grad = (hidden_grad * act_slope).astype(jnp.bfloat16)
        sum_bias[...] += jnp.sum(pre_grad.astype(jnp.float32), axis=0, keepdims=True)
        hidden, pre_grad = hidden.T, pre_grad.T
        for j in range(2):
            columns = pl.ds(pl.multiple_of((own ^ j) * width, width), width)
            sum_in[j] += jnp.dot(pre_grad, features[here, columns], preferred_element_type=jnp.float32)
            sum_out[j] += jnp.dot(hidden, cotangent[here, columns], preferred_element_type=jnp.float32)

    grad_in[...] = sum_in[0].T
    grad_out[...] = sum_out[0]
    end_grads[:width, :] = sum_in[1].T.astype(jnp.bfloat16)
    for q in range(width // size):
        end_grads[width + q * size : width + (q + 1) * size, :] = sum_out[1, :, q * size : (q + 1) * size].astype(jnp.bfloat16)
    grad_bias[...] = sum_bias[...]
    part_rows = lax.broadcasted_iota(jnp.int32, (BIAS_ROWS, size), 0)
    rest = sum_bias[...]
    parts = jnp.zeros((BIAS_ROWS, size), jnp.float32)
    for i in range(3):
        rounded = rest.astype(jnp.bfloat16).astype(jnp.float32)
        parts = jnp.where(part_rows == i, rounded, parts)
        rest = rest - rounded
    end_grads[2 * width :, :] = parts.astype(jnp.bfloat16)


def hidden_chunk(chunk, scalars, features, cotangents, own_weights, fars, bias):
    groups, pieces = len(features), len(features[0])
    rows, width = features[0][0].shape
    size = HIDDEN_CHUNK
    flat = [piece for group in features for piece in group] + [piece for group in cotangents for piece in group]
    flat += [*own_weights] + [array for array, _ in fars]

    def whole(array):
        return pl.BlockSpec(array.shape, lambda i, s: (0,) * array.ndim)

    shapes = [
        jax.ShapeDtypeStruct((width, size), jnp.float32),
        jax.ShapeDtypeStruct((size, width), jnp.float32),
        jax.ShapeDtypeStruct((2 * width + BIAS_ROWS, size), jnp.bfloat16),
        jax.ShapeDtypeStruct((1, size), jnp.float32),
    ]
    return pl.pallas_call(
        functools.partial(chunk_kernel, chunk, pieces, [place for _, place in fars]),
        out_shape=shapes,
        grid_spec=pltpu.PrefetchScalarGridSpec(
            num_scalar_prefetch=1,
            grid=(1,),
            in_specs=[pl.BlockSpec(memory_space=pl.ANY)] * len(flat) + [pl.BlockSpec((1, size), lambda i, s: (0, chunk))],
            out_specs=[whole(shape) for shape in shapes],
            scratch_shapes=[
                pltpu.VMEM((groups * rows, pieces * width), jnp.bfloat16),
                pltpu.VMEM((groups * rows, pieces * width), jnp.bfloat16),
                pltpu.VMEM((pieces * width, size), jnp.bfloat16),
                pltpu.VMEM((pieces * width, size), jnp.bfloat16),
                pltpu.VMEM((2, size, width), jnp.float32),
                pltpu.VMEM((2, size, width), jnp.float32),
                pltpu.VMEM((1, size), jnp.float32),
                pltpu.SemaphoreType.DMA((2, groups * rows // ROW_TILE, pieces)),
                pltpu.SemaphoreType.DMA((2, pieces)),
            ],
        ),
        compiler_params=pltpu.CompilerParams(vmem_limit_bytes=VMEM_BYTES),
        cost_estimate=pl.CostEstimate(
            flops=2 * 2 * groups * rows * (pieces + 2) * width * size,
            bytes_accessed=2 * 2 * groups * pieces * rows * width,
            transcendentals=groups * rows * size,
        ),
        name=f"hidden_chunk_{chunk}",
    )(scalars, *flat, bias)


def pack_kernel(half, blocks, slot_of, filled, masks, numbers, sent):
    slots_per = masks.shape[0] // blocks
    planes = sent.shape[0]

    @pl.loop(0, planes * half)
    def _(place):
        row = pl.multiple_of(lax.rem(place, half) * TILE_SIZE, TILE_SIZE)
        sent[place // half, pl.ds(row, TILE_SIZE), :] = (masks[slot_of[place]] * filled[place]).astype(sent.dtype)

    row_ids = lax.broadcasted_iota(jnp.int32, (HEADER_ROWS, TILE_SIZE), 0)
    ones = jnp.ones((HEADER_ROWS, TILE_SIZE), jnp.bfloat16)
    header = jnp.zeros((HEADER_ROWS, TILE_SIZE), jnp.float32)
    for block in range(blocks):
        total = masks[block * slots_per]
        for slot in range(1, slots_per):
            total += masks[block * slots_per + slot]
        counts = lax.dot_general(
            ones, total.astype(jnp.bfloat16), (((1,), (1,)), ((), ())), preferred_element_type=jnp.float32
        ).astype(jnp.int32)
        header = jnp.where(row_ids == 1 + block, (counts // TILE_SIZE).astype(jnp.float32), header)
        header = jnp.where(row_ids == 1 + blocks + block, (counts % TILE_SIZE).astype(jnp.float32), header)
    for plane in range(planes):
        own_numbers = numbers[plane : plane + 1, :].astype(jnp.float32)
        sent[plane, half * TILE_SIZE :, :] = jnp.where(row_ids == 0, own_numbers, header).astype(sent.dtype)


def pack_masks(slot_of, filled, masks, numbers, blocks):
    planes, half = slot_of.shape
    shape = jax.ShapeDtypeStruct((planes, half * TILE_SIZE + HEADER_ROWS, TILE_SIZE), jnp.bfloat16)
    return pl.pallas_call(
        functools.partial(pack_kernel, half, blocks),
        out_shape=shape,
        grid_spec=pltpu.PrefetchScalarGridSpec(
            num_scalar_prefetch=2,
            grid=(1,),
            in_specs=[
                pl.BlockSpec(masks.shape, lambda i, s, f: (0, 0, 0)),
                pl.BlockSpec(numbers.shape, lambda i, s, f: (0, 0)),
            ],
            out_specs=pl.BlockSpec(shape.shape, lambda i, s, f: (0, 0, 0)),
        ),
        compiler_params=pltpu.CompilerParams(vmem_limit_bytes=VMEM_BYTES),
        name="pack_masks",
    )(slot_of.reshape(-1), filled.astype(jnp.int32).reshape(-1), masks, numbers)


def middle_planes(previous_embedding, tile_source, tile_mask, row_order, w_in, b_in, w_out, grad_out):
    plane, part, core = lax.axis_index("vocab"), lax.axis_index("groups"), lax.axis_index("sub")
    column = 2 * lax.axis_index("mp") + core
    planes = lax.axis_size("vocab")
    blocks, slots_per = tile_source.shape
    total_slots = blocks * slots_per
    tiles_here = previous_embedding.shape[0] // TILE_SIZE
    columns = previous_embedding.shape[1]
    tile_lookup = previous_embedding.reshape(tiles_here, TILE_SIZE, columns)
    rows = row_order.shape[0]
    places = 2 * total_slots // planes
    half = places // 2
    bf16, f32 = jnp.bfloat16, jnp.float32

    def to_middle(array):
        return lax.ppermute(array, "vocab", TO_MIDDLE)

    def across(array):
        return lax.ppermute(array, "vocab", ACROSS)

    def to_end(array):
        return lax.ppermute(array, "vocab", TO_END)

    def swap_x(array):
        return lax.ppermute(array, "mp", SWAP)

    def swap_y(array):
        return lax.ppermute(array, "groups", SWAP)

    def swap_core(array):
        return lax.ppermute(array, "sub", SWAP)

    source = tile_source.reshape(-1)
    owner = source // tiles_here
    slot_ids = jnp.arange(total_slots)
    earlier = slot_ids[None, :] < slot_ids[:, None]
    position = jnp.sum(jnp.where(earlier & (owner[None, :] == owner[:, None]), 1, 0), axis=1)
    my_places = core * half + jnp.arange(half)
    hit = (owner[:, None, None] == jnp.arange(planes)[None, :, None]) & (
        position[:, None, None] == my_places[None, None, :]
    )
    slot_of = jnp.sum(jnp.where(hit, slot_ids[:, None, None], 0), axis=0)
    filled = jnp.any(hit, axis=0)
    numbers = jnp.concatenate(
        [
            jnp.sum(jnp.where(hit, (source % tiles_here)[:, None, None], 0), axis=0),
            jnp.sum(jnp.where(hit, (slot_ids // slots_per)[:, None, None], 0), axis=0),
        ],
        axis=1,
    )
    numbers = jnp.pad(numbers, ((0, 0), (0, TILE_SIZE - 2 * half)))
    masks = tile_mask.reshape(total_slots, TILE_SIZE, TILE_SIZE)
    sent = pack_masks(slot_of, filled, masks, numbers, blocks)

    placed = (row_order % rows)[None, :] == jnp.arange(rows)[:, None]
    cot = jnp.dot(placed.astype(bf16), grad_out, preferred_element_type=f32).astype(bf16)

    hidden_units, width = w_out.shape
    size = HIDDEN_CHUNK
    w_out_t = w_out.T
    my_weights = jnp.where(part == 0, w_in, w_out_t)

    def my_half(chunk):
        return my_weights[:, chunk * size : (chunk + 1) * size]

    def both(a, b):
        return (a.astype(f32) + b.astype(f32)).astype(bf16)

    def mixed_of(group, side, other):
        return ((side.astype(f32) + other.astype(f32)) * all_inverse[group][:, None]).astype(bf16)

    def partial_of(group, ids):
        return mix_group(group, rows, places, ids, block_ids, tile_lookup, masks, sibling)

    def numbers_of(array):
        header = array[:, half * TILE_SIZE, : 2 * half].astype(jnp.int32)
        return header[:, :half], header[:, half:]

    own01 = jnp.stack([my_half(0), my_half(1)])
    own23 = jnp.stack([my_half(2), my_half(3)])
    got = lax.all_to_all(sent, "vocab", split_axis=0, concat_axis=0, tiled=True)
    cot_x = swap_x(cot)

    masks, cot, cot_x, own01, own23 = gated((got, cot, cot_x, own01, own23), ())
    sibling = swap_core(masks)
    cot_far = across(cot)
    r01 = across(own01)
    cot_end = to_middle(cot)
    cot_s, cot_xs = swap_core(cot), swap_core(cot_x)
    own_numbers, sibling_numbers = numbers_of(masks), numbers_of(sibling)
    tile_ids, block_ids = (jnp.concatenate(pair, axis=1).reshape(-1) for pair in zip(own_numbers, sibling_numbers))
    first = half * TILE_SIZE + 1
    count_high, count_low = (masks[:, first + i * blocks : first + (i + 1) * blocks].astype(f32) for i in range(2))
    all_inverse = (1.0 / jnp.maximum(count_high * TILE_SIZE + count_low, 1.0)).reshape(planes, rows)
    p0 = partial_of(0, tile_ids)

    p0, cot_end, cot_far, ids = gated((p0, cot_end, cot_far, tile_ids), (cot_s, cot_xs, all_inverse))
    a0 = to_middle(p0)
    cot_end_x = swap_x(cot_end)
    p1, p2, p3 = (partial_of(group, ids) for group in range(1, planes))
    cot_end_s, cot_far_s = swap_core(cot_end), swap_core(cot_far)
    cot_end, p1, p2, p3 = gated((cot_end, p1, p2, p3), ())
    cot_far_end = across(cot_end)

    p1, p0, a0, cot_far, r01, cot_end_x = gated((p1, p0, a0, cot_far, r01, cot_end_x), (cot_end_s, cot_far_s))
    a1 = to_middle(p1)
    s0 = both(p0, a0)
    o0 = across(s0)
    cot_far_x = swap_x(cot_far)
    y01 = swap_y(r01)
    cot_end_xs = swap_core(cot_end_x)

    p2, p1, a1, cot_far_x, cot_far_end = gated((p2, p1, a1, cot_far_x, cot_far_end), (cot_end_xs, y01))
    a2 = to_middle(p2)
    s1 = both(p1, a1)
    o1 = across(s1)
    cot_far_end_x = swap_x(cot_far_end)
    cot_far_xs, cot_far_end_s = swap_core(cot_far_x), swap_core(cot_far_end)

    f0 = mixed_of(0, s0, o0)
    p3, p2, a2, f0, cot_far_end_x = gated((p3, p2, a2, f0, cot_far_end_x), (cot_far_xs, cot_far_end_s))
    f0_x = swap_x(f0)
    a3 = to_middle(p3)
    s2 = both(p2, a2)
    o2 = across(s2)
    f0_s, cot_far_end_xs = swap_core(f0), swap_core(cot_far_end_x)

    f1 = mixed_of(1, s1, o1)
    f1, f0_x = gated((f1, f0_x), (f0_s, cot_far_end_xs))
    f1_x = swap_x(f1)
    p3, a3, own01 = gated((p3, a3, own01), ())
    e01 = to_middle(own01)
    s3 = both(p3, a3)
    o3 = across(s3)
    f1_s, f0_xs = swap_core(f1), swap_core(f0_x)

    f2 = mixed_of(2, s2, o2)
    f2, f1_x = gated((f2, f1_x), (f1_s, f0_xs))
    f2_x = swap_x(f2)
    e01, o2 = gated((e01, o2), ())
    r_e01 = across(e01)
    ye01 = swap_y(e01)
    f2_s, f1_xs = swap_core(f2), swap_core(f1_x)

    f3 = mixed_of(3, s3, o3)
    f3, f2_x, own23 = gated((f3, f2_x, own23), (f2_s, f1_xs, ye01))
    f3_x = swap_x(f3)
    e23 = to_middle(own23)
    f3_s, f2_xs = swap_core(f3), swap_core(f2_x)
    r_e01, f3_s = gated((r_e01, f3_s), (f2_xs,))
    y_e01 = swap_y(r_e01)

    f3_x, y_e01 = gated((f3_x, y_e01), (f3_s,))
    f3_xs = swap_core(f3_x)
    r2 = across(jnp.stack([own23[0], e23[0]]))
    r3 = across(jnp.stack([own23[1], e23[1]]))
    ye23 = swap_y(e23)
    features = [[f0, f0_s, f0_x, f0_xs], [f1, f1_s, f1_x, f1_xs], [f2, f2_s, f2_x, f2_xs], [f3, f3_s, f3_x, f3_xs]]
    cotangents = [
        [cot, cot_s, cot_x, cot_xs],
        [cot_end, cot_end_s, cot_end_x, cot_end_xs],
        [cot_far_end, cot_far_end_s, cot_far_end_x, cot_far_end_xs],
        [cot_far, cot_far_s, cot_far_x, cot_far_xs],
    ]
    scalars = jnp.stack([plane ^ column, part, plane]).astype(jnp.int32)
    bias = b_in.reshape(1, -1)

    def run(chunk, *moved):
        return hidden_chunk(chunk, scalars, features, cotangents, (w_in, w_out_t), *moved, bias)

    g0 = run(0, [(r01, 0), (r_e01, 0), (e01, 0), (y01, 0), (y_e01, 0), (ye01, 0)])

    r2, end0 = gated((r2, g0[2]), ())
    y2 = swap_y(r2)
    c0 = to_end(end0)
    g1 = run(1, [(r01, 1), (r_e01, 1), (e01, 1), (y01, 1), (y_e01, 1), (ye01, 1)])

    r3, y2, end1, c0 = gated((r3, y2, g1[2], c0), (ye23,))
    y3 = swap_y(r3)
    c1 = to_end(end1)
    g2 = run(2, [(r2, 0), (r2, 1), (e23, 0), (y2, 0), (y2, 1), (ye23, 0)])

    y3, end2, c1 = gated((y3, g2[2], c1), ())
    c2 = to_end(end2)
    g3 = run(3, [(r3, 0), (r3, 1), (e23, 1), (y3, 0), (y3, 1), (ye23, 1)])
    end3, c0, c1, c2 = gated((g3[2], c0, c1, c2), ())
    c3 = to_end(end3)

    is_middle = (plane == 1) | (plane == 2)
    grad_w_in = jnp.zeros((width, hidden_units), f32)
    grad_w_out = jnp.zeros((hidden_units, width), f32)
    biases = []
    for chunk, ((own_in, own_out, _, own_bias), end) in enumerate(zip((g0, g1, g2, g3), (c0, c1, c2, c3))):
        end = end.astype(f32)
        here = slice(chunk * size, (chunk + 1) * size)
        end_out = end[width : 2 * width].reshape(width // size, size, size).transpose(1, 0, 2).reshape(size, width)
        grad_w_in = grad_w_in.at[:, here].set(jnp.where(is_middle, own_in, end[:width]))
        grad_w_out = grad_w_out.at[here].set(jnp.where(is_middle, own_out, end_out))
        high, middle, low = (end[2 * width + i] for i in range(3))
        biases.append(jnp.where(is_middle, own_bias[0], (high + middle) + low))
    return (grad_w_in, grad_w_out, jnp.concatenate(biases))


def gathered(previous_embedding, tile_source, tile_mask, row_order, w_in, b_in, w_out, grad_out):
    groups = lax.axis_size("vocab")
    blocks, slots_per = tile_source.shape
    tiles_here = previous_embedding.shape[0] // TILE_SIZE
    columns = previous_embedding.shape[1]
    flat_source = tile_source.reshape(-1)
    owner_dev = flat_source // tiles_here
    local_tile = flat_source % tiles_here
    total_slots = flat_source.shape[0]
    capacity = max(2, 2 * total_slots // groups)
    slot_ids = jnp.arange(total_slots)
    earlier = slot_ids[None, :] < slot_ids[:, None]
    same_owner = owner_dev[None, :] == owner_dev[:, None]
    position = jnp.sum(jnp.where(earlier & same_owner, 1, 0), axis=1).astype(jnp.int32)
    owner_hit = owner_dev[:, None] == jnp.arange(groups)[None, :]
    place_hit = position[:, None] == jnp.arange(capacity)[None, :]
    placed = owner_hit[:, :, None] & place_hit[:, None, :]
    slot_index = owner_dev * capacity + position
    mask_values = tile_mask.astype(jnp.bfloat16)
    requests = jnp.sum(jnp.where(placed, local_tile[:, None, None], 0), axis=0)
    tile_lookup = previous_embedding.reshape(tiles_here, TILE_SIZE, columns)
    found_tiles = jnp.take(
        tile_lookup,
        lax.all_to_all(requests, "vocab", split_axis=0, concat_axis=0, tiled=True),
        axis=0,
    )
    arrived = lax.all_to_all(found_tiles, "vocab", split_axis=0, concat_axis=0, tiled=True)
    picked = arrived.reshape(groups * capacity, TILE_SIZE, columns)[slot_index]
    picked = picked.reshape(blocks, slots_per, TILE_SIZE, columns)
    summed = jnp.einsum("bkrc,bkcd->brd", mask_values, picked, preferred_element_type=jnp.float32)
    counts = jnp.sum(tile_mask, axis=(1, 3))
    inverse = 1.0 / jnp.maximum(counts, 1).astype(jnp.float32)
    mixed = (summed * inverse[:, :, None]).astype(jnp.bfloat16).reshape(blocks * TILE_SIZE, columns)
    rows_here = mixed.shape[0]
    ordered = mixed[row_order % rows_here]
    w_in_full = lax.all_gather(w_in, "vocab", axis=0, tiled=True)
    features = lax.all_gather(ordered, ("mp", "sub"), axis=1, tiled=True)
    preact = jnp.dot(features, w_in_full, preferred_element_type=jnp.float32) + b_in
    activation, act_slope = gelu_parts(preact)
    hidden = activation.astype(jnp.bfloat16)
    w_out_full = lax.all_gather(w_out, "vocab", axis=1, tiled=True)
    cotangent = lax.all_gather(grad_out, ("mp", "sub"), axis=1, tiled=True)
    hidden_grad = lax.dot_general(
        cotangent, w_out_full, (((1,), (1,)), ((), ())), preferred_element_type=jnp.float32
    )
    pre_grad = (hidden_grad * act_slope).astype(jnp.bfloat16)
    grad_bias = lax.psum(jnp.sum(pre_grad.astype(jnp.float32), axis=0), "vocab")
    grad_w_in = lax.psum_scatter(
        lax.dot_general(
            features, pre_grad, (((0,), (0,)), ((), ())), preferred_element_type=jnp.float32
        ).astype(jnp.bfloat16),
        "vocab",
        scatter_dimension=0,
        tiled=True,
    ).astype(jnp.float32)
    grad_w_out = (
        lax.psum_scatter(
            lax.dot_general(
                cotangent, hidden, (((0,), (0,)), ((), ())), preferred_element_type=jnp.float32
            ).astype(jnp.bfloat16),
            "vocab",
            scatter_dimension=0,
            tiled=True,
        )
        .astype(jnp.float32)
        .T
    )
    return (grad_w_in, grad_w_out, grad_bias)


def solution(mesh):
    placed = (
        P("vocab", ("mp", "sub")),
        P(("groups", "vocab"), None),
        P(("groups", "vocab"), None, None, None),
        P(("groups", "vocab")),
        P("vocab", ("mp", "sub")),
        P(("mp", "sub")),
        P(("mp", "sub"), "vocab"),
        P(("groups", "vocab"), ("mp", "sub")),
    )
    return jax.shard_map(
        middle_planes if planes_fit(mesh) else gathered,
        mesh=mesh,
        in_specs=placed,
        out_specs=(
            P(("groups", "vocab"), ("mp", "sub")),
            P(("groups", "mp", "sub"), "vocab"),
            P(("groups", "mp", "sub")),
        ),
        check_vma=False,
    )
```

```python
import functools

import jax
import jax.numpy as jnp
from jax import lax
from jax.experimental import pallas as pl
from jax.experimental.pallas import tpu as pltpu
from jax.sharding import PartitionSpec as P

TILE_SIZE = 128


tanh_scale = 0.7978845608028654
cubic_term = 0.044715


def gelu_parts(values):
    inner_arg = tanh_scale * (values + cubic_term * values * values * values)
    tangent = jnp.tanh(inner_arg)
    activation = 0.5 * values * (1.0 + tangent)
    act_slope = 0.5 * (1.0 + tangent) + 0.5 * values * (1.0 - tangent * tangent) * tanh_scale * (
        1.0 + 3.0 * cubic_term * values * values
    )
    return (activation, act_slope)


TO_MIDDLE = [(0, 1), (3, 2)]
ACROSS = [(1, 2), (2, 1)]
TO_END = [(1, 0), (2, 3)]
SWAP = [(0, 1), (1, 0)]

ROW_TILE = 512
AHEAD = 1
HIDDEN_CHUNK = 256
HEADER_ROWS = 16
BIAS_ROWS = 16
VMEM_BYTES = 60 * 1024 * 1024


def planes_fit(mesh):
    return dict(mesh.shape) == dict(groups=2, vocab=4, mp=2, sub=2)


def gated(values, results):
    return lax.optimization_barrier((tuple(values), tuple(results)))[0]


def mix_kernel(group, places, tile_ids, block_ids, *refs):
    tiles, (own_masks, sibling_masks, out, total) = refs[:places], refs[places:]
    total[...] = jnp.zeros_like(total)
    half = places // 2
    for place in range(places):
        masks = own_masks if place < half else sibling_masks
        mask = masks[0, (place % half) * TILE_SIZE : (place % half + 1) * TILE_SIZE, :]
        start = pl.multiple_of(block_ids[group * places + place] * TILE_SIZE, TILE_SIZE)
        total[pl.ds(start, TILE_SIZE), :] += jnp.dot(mask, tiles[place][0], preferred_element_type=jnp.float32)
    out[...] = total[...].astype(out.dtype)


def mix_group(group, rows, places, tile_ids, block_ids, tile_lookup, own_masks, sibling_masks):
    columns = tile_lookup.shape[2]

    def tile_spec(place):
        return pl.BlockSpec((1, TILE_SIZE, columns), lambda i, ids, blocks: (ids[group * places + place], 0, 0))

    mask_spec = pl.BlockSpec((1,) + own_masks.shape[1:], lambda i, ids, blocks: (group, 0, 0))
    return pl.pallas_call(
        functools.partial(mix_kernel, group, places),
        out_shape=jax.ShapeDtypeStruct((rows, columns), jnp.bfloat16),
        grid_spec=pltpu.PrefetchScalarGridSpec(
            num_scalar_prefetch=2,
            grid=(1,),
            in_specs=[tile_spec(place) for place in range(places)] + [mask_spec] * 2,
            out_specs=pl.BlockSpec((rows, columns), lambda i, ids, blocks: (0, 0)),
            scratch_shapes=[pltpu.VMEM((rows, columns), jnp.float32)],
        ),
        compiler_params=pltpu.CompilerParams(vmem_limit_bytes=VMEM_BYTES),
        cost_estimate=pl.CostEstimate(
            flops=2 * places * TILE_SIZE * TILE_SIZE * columns,
            bytes_accessed=2 * places * TILE_SIZE * columns + 2 * rows * columns,
            transcendentals=0,
        ),
        name=f"mix_group_{group}",
    )(tile_ids, block_ids, *([tile_lookup] * places), own_masks, sibling_masks)


def chunk_kernel(chunk, pieces, far_places, scalars, *refs):
    feature_refs = [refs[g * pieces : (g + 1) * pieces] for g in range(4)]
    cotangent_refs = [refs[(4 + g) * pieces : (5 + g) * pieces] for g in range(4)]
    (own_in, own_out, *fars, bias, grad_in, grad_out, end_grads, grad_bias,
     features, cotangent, in_all, out_all, sum_in, sum_out, sum_bias, held, sems, weight_sems) = refs[8 * pieces :]
    fars = [far if place is None else far.at[place] for far, place in zip(fars, far_places)]
    own, part, plane = scalars[0], scalars[1], scalars[2]
    size = in_all.shape[1]
    rows, width = feature_refs[0][0].shape
    tiles = rows // ROW_TILE

    def weights(source, target, k, kind):
        target = target.at[pl.ds(pl.multiple_of((own ^ k) * width, width), width)]
        return pltpu.make_async_copy(source, target, weight_sems.at[kind, k])

    for kind, (source, target) in enumerate(((own_in, in_all), (own_out, out_all))):
        weights(source.at[:, pl.ds(chunk * size, size)], target, 0, kind).start()
    for half in range(2):

        @pl.when(part == half)
        def _():
            for i, k in ((0, 3), (1, 2), (2, 1)):
                weights(fars[3 * half + i], in_all, k, 0).start()
                weights(fars[3 - 3 * half + i], out_all, k, 1).start()

    def move(source, target, kind, step, tile, k):
        from_rows = pl.ds(pl.multiple_of(tile * ROW_TILE, ROW_TILE), ROW_TILE)
        to_rows = pl.ds(pl.multiple_of(step * ROW_TILE, ROW_TILE), ROW_TILE)
        return pltpu.make_async_copy(
            source.at[from_rows], target.at[to_rows, pl.ds(k * width, width)], sems.at[kind, step, k]
        )

    def fetch(step):
        group, tile = step // tiles, step % tiles
        for i in range(4):

            @pl.when(group == i)
            def _():
                for k in range(pieces):
                    move(feature_refs[i][k], features, 0, step, tile, k).start()

            @pl.when((plane ^ group) == i)
            def _():
                for k in range(pieces):
                    move(cotangent_refs[i][k], cotangent, 1, step, tile, k).start()

    for step in range(AHEAD):
        fetch(step)
    sum_in[...] = jnp.zeros_like(sum_in)
    sum_out[...] = jnp.zeros_like(sum_out)
    sum_bias[...] = jnp.zeros_like(sum_bias)
    for k in range(pieces):
        weights(fars[0], in_all, k, 0).wait()
        weights(fars[0], out_all, k, 1).wait()

    def forward(step):
        here = pl.ds(pl.multiple_of(step * ROW_TILE, ROW_TILE), ROW_TILE)
        for k in range(pieces):
            move(feature_refs[0][k], features, 0, step, 0, k).wait()
            move(cotangent_refs[0][k], cotangent, 1, step, 0, k).wait()
        preact = bias[...] + jnp.dot(features[here, :], in_all[...], preferred_element_type=jnp.float32)
        hidden_grad = jnp.dot(cotangent[here, :], out_all[...], preferred_element_type=jnp.float32)
        activation, act_slope = gelu_parts(preact)
        hidden = activation.astype(jnp.bfloat16)
        pre_grad = (hidden_grad * act_slope).astype(jnp.bfloat16)
        sum_bias[...] += jnp.sum(pre_grad.astype(jnp.float32), axis=0, keepdims=True)
        return hidden.T, pre_grad.T

    def backward(step, hidden, pre_grad):
        here = pl.ds(pl.multiple_of(step * ROW_TILE, ROW_TILE), ROW_TILE)
        for j in range(2):
            columns = pl.ds(pl.multiple_of((own ^ j) * width, width), width)
            sum_in[j] += jnp.dot(pre_grad, features[here, columns], preferred_element_type=jnp.float32)
            sum_out[j] += jnp.dot(hidden, cotangent[here, columns], preferred_element_type=jnp.float32)

    last = 4 * tiles - 1
    fetch(1)
    held[0], held[1] = forward(0)

    @pl.loop(1, last + 1)
    def _(step):
        @pl.when(step < last)
        def _():
            fetch(step + 1)

        hidden, pre_grad = held[0], held[1]
        new_hidden, new_pre_grad = forward(step)
        backward(step - 1, hidden, pre_grad)
        held[0], held[1] = new_hidden, new_pre_grad

    backward(last, held[0], held[1])

    grad_in[...] = sum_in[0].T
    grad_out[...] = sum_out[0]
    end_grads[:width, :] = sum_in[1].T.astype(jnp.bfloat16)
    for q in range(width // size):
        end_grads[width + q * size : width + (q + 1) * size, :] = sum_out[1, :, q * size : (q + 1) * size].astype(jnp.bfloat16)
    grad_bias[...] = sum_bias[...]
    part_rows = lax.broadcasted_iota(jnp.int32, (BIAS_ROWS, size), 0)
    rest = sum_bias[...]
    parts = jnp.zeros((BIAS_ROWS, size), jnp.float32)
    for i in range(3):
        rounded = rest.astype(jnp.bfloat16).astype(jnp.float32)
        parts = jnp.where(part_rows == i, rounded, parts)
        rest = rest - rounded
    end_grads[2 * width :, :] = parts.astype(jnp.bfloat16)


def hidden_chunk(chunk, scalars, features, cotangents, own_weights, fars, bias):
    groups, pieces = len(features), len(features[0])
    rows, width = features[0][0].shape
    size = HIDDEN_CHUNK
    flat = [piece for group in features for piece in group] + [piece for group in cotangents for piece in group]
    flat += [*own_weights] + [array for array, _ in fars]

    def whole(array):
        return pl.BlockSpec(array.shape, lambda i, s: (0,) * array.ndim)

    shapes = [
        jax.ShapeDtypeStruct((width, size), jnp.float32),
        jax.ShapeDtypeStruct((size, width), jnp.float32),
        jax.ShapeDtypeStruct((2 * width + BIAS_ROWS, size), jnp.bfloat16),
        jax.ShapeDtypeStruct((1, size), jnp.float32),
    ]
    return pl.pallas_call(
        functools.partial(chunk_kernel, chunk, pieces, [place for _, place in fars]),
        out_shape=shapes,
        grid_spec=pltpu.PrefetchScalarGridSpec(
            num_scalar_prefetch=1,
            grid=(1,),
            in_specs=[pl.BlockSpec(memory_space=pl.ANY)] * len(flat) + [pl.BlockSpec((1, size), lambda i, s: (0, chunk))],
            out_specs=[whole(shape) for shape in shapes],
            scratch_shapes=[
                pltpu.VMEM((groups * rows, pieces * width), jnp.bfloat16),
                pltpu.VMEM((groups * rows, pieces * width), jnp.bfloat16),
                pltpu.VMEM((pieces * width, size), jnp.bfloat16),
                pltpu.VMEM((pieces * width, size), jnp.bfloat16),
                pltpu.VMEM((2, size, width), jnp.float32),
                pltpu.VMEM((2, size, width), jnp.float32),
                pltpu.VMEM((1, size), jnp.float32),
                pltpu.VMEM((2, size, ROW_TILE), jnp.bfloat16),
                pltpu.SemaphoreType.DMA((2, groups * rows // ROW_TILE, pieces)),
                pltpu.SemaphoreType.DMA((2, pieces)),
            ],
        ),
        compiler_params=pltpu.CompilerParams(vmem_limit_bytes=VMEM_BYTES),
        cost_estimate=pl.CostEstimate(
            flops=2 * 2 * groups * rows * (pieces + 2) * width * size,
            bytes_accessed=2 * 2 * groups * pieces * rows * width,
            transcendentals=groups * rows * size,
        ),
        name=f"hidden_chunk_{chunk}",
    )(scalars, *flat, bias)


def pack_kernel(half, blocks, slot_of, filled, masks, numbers, sent):
    slots_per = masks.shape[0] // blocks
    planes = sent.shape[0]

    @pl.loop(0, planes * half)
    def _(place):
        row = pl.multiple_of(lax.rem(place, half) * TILE_SIZE, TILE_SIZE)
        sent[place // half, pl.ds(row, TILE_SIZE), :] = (masks[slot_of[place]] * filled[place]).astype(sent.dtype)

    row_ids = lax.broadcasted_iota(jnp.int32, (HEADER_ROWS, TILE_SIZE), 0)
    ones = jnp.ones((HEADER_ROWS, TILE_SIZE), jnp.bfloat16)
    header = jnp.zeros((HEADER_ROWS, TILE_SIZE), jnp.float32)
    for block in range(blocks):
        total = masks[block * slots_per]
        for slot in range(1, slots_per):
            total += masks[block * slots_per + slot]
        counts = lax.dot_general(
            ones, total.astype(jnp.bfloat16), (((1,), (1,)), ((), ())), preferred_element_type=jnp.float32
        ).astype(jnp.int32)
        header = jnp.where(row_ids == 1 + block, (counts // TILE_SIZE).astype(jnp.float32), header)
        header = jnp.where(row_ids == 1 + blocks + block, (counts % TILE_SIZE).astype(jnp.float32), header)
    for plane in range(planes):
        own_numbers = numbers[plane : plane + 1, :].astype(jnp.float32)
        sent[plane, half * TILE_SIZE :, :] = jnp.where(row_ids == 0, own_numbers, header).astype(sent.dtype)


def pack_masks(slot_of, filled, masks, numbers, blocks):
    planes, half = slot_of.shape
    shape = jax.ShapeDtypeStruct((planes, half * TILE_SIZE + HEADER_ROWS, TILE_SIZE), jnp.bfloat16)
    return pl.pallas_call(
        functools.partial(pack_kernel, half, blocks),
        out_shape=shape,
        grid_spec=pltpu.PrefetchScalarGridSpec(
            num_scalar_prefetch=2,
            grid=(1,),
            in_specs=[
                pl.BlockSpec(masks.shape, lambda i, s, f: (0, 0, 0)),
                pl.BlockSpec(numbers.shape, lambda i, s, f: (0, 0)),
            ],
            out_specs=pl.BlockSpec(shape.shape, lambda i, s, f: (0, 0, 0)),
        ),
        compiler_params=pltpu.CompilerParams(vmem_limit_bytes=VMEM_BYTES),
        name="pack_masks",
    )(slot_of.reshape(-1), filled.astype(jnp.int32).reshape(-1), masks, numbers)


def middle_planes(previous_embedding, tile_source, tile_mask, row_order, w_in, b_in, w_out, grad_out):
    plane, part, core = lax.axis_index("vocab"), lax.axis_index("groups"), lax.axis_index("sub")
    column = 2 * lax.axis_index("mp") + core
    planes = lax.axis_size("vocab")
    blocks, slots_per = tile_source.shape
    total_slots = blocks * slots_per
    tiles_here = previous_embedding.shape[0] // TILE_SIZE
    columns = previous_embedding.shape[1]
    tile_lookup = previous_embedding.reshape(tiles_here, TILE_SIZE, columns)
    rows = row_order.shape[0]
    places = 2 * total_slots // planes
    half = places // 2
    bf16, f32 = jnp.bfloat16, jnp.float32

    def to_middle(array):
        return lax.ppermute(array, "vocab", TO_MIDDLE)

    def across(array):
        return lax.ppermute(array, "vocab", ACROSS)

    def to_end(array):
        return lax.ppermute(array, "vocab", TO_END)

    def swap_x(array):
        return lax.ppermute(array, "mp", SWAP)

    def swap_y(array):
        return lax.ppermute(array, "groups", SWAP)

    def swap_core(array):
        return lax.ppermute(array, "sub", SWAP)

    source = tile_source.reshape(-1)
    owner = source // tiles_here
    slot_ids = jnp.arange(total_slots)
    earlier = slot_ids[None, :] < slot_ids[:, None]
    position = jnp.sum(jnp.where(earlier & (owner[None, :] == owner[:, None]), 1, 0), axis=1)
    my_places = core * half + jnp.arange(half)
    hit = (owner[:, None, None] == jnp.arange(planes)[None, :, None]) & (
        position[:, None, None] == my_places[None, None, :]
    )
    slot_of = jnp.sum(jnp.where(hit, slot_ids[:, None, None], 0), axis=0)
    filled = jnp.any(hit, axis=0)
    numbers = jnp.concatenate(
        [
            jnp.sum(jnp.where(hit, (source % tiles_here)[:, None, None], 0), axis=0),
            jnp.sum(jnp.where(hit, (slot_ids // slots_per)[:, None, None], 0), axis=0),
        ],
        axis=1,
    )
    numbers = jnp.pad(numbers, ((0, 0), (0, TILE_SIZE - 2 * half)))
    masks = tile_mask.reshape(total_slots, TILE_SIZE, TILE_SIZE)
    sent = pack_masks(slot_of, filled, masks, numbers, blocks)

    placed = (row_order % rows)[None, :] == jnp.arange(rows)[:, None]
    cot = jnp.dot(placed.astype(bf16), grad_out, preferred_element_type=f32).astype(bf16)

    hidden_units, width = w_out.shape
    size = HIDDEN_CHUNK
    w_out_t = w_out.T
    my_weights = jnp.where(part == 0, w_in, w_out_t)

    def my_half(chunk):
        return my_weights[:, chunk * size : (chunk + 1) * size]

    def both(a, b):
        return (a.astype(f32) + b.astype(f32)).astype(bf16)

    def mixed_of(group, side, other):
        return ((side.astype(f32) + other.astype(f32)) * all_inverse[group][:, None]).astype(bf16)

    def partial_of(group, ids):
        return mix_group(group, rows, places, ids, block_ids, tile_lookup, masks, sibling)

    def numbers_of(array):
        header = array[:, half * TILE_SIZE, : 2 * half].astype(jnp.int32)
        return header[:, :half], header[:, half:]

    own01 = jnp.stack([my_half(0), my_half(1)])
    own23 = jnp.stack([my_half(2), my_half(3)])
    got = lax.all_to_all(sent, "vocab", split_axis=0, concat_axis=0, tiled=True)
    cot_x = swap_x(cot)

    masks, cot, cot_x, own01, own23 = gated((got, cot, cot_x, own01, own23), ())
    sibling = swap_core(masks)
    cot_far = across(cot)
    r01 = across(own01)
    cot_end = to_middle(cot)
    cot_s, cot_xs = swap_core(cot), swap_core(cot_x)
    own_numbers, sibling_numbers = numbers_of(masks), numbers_of(sibling)
    tile_ids, block_ids = (jnp.concatenate(pair, axis=1).reshape(-1) for pair in zip(own_numbers, sibling_numbers))
    first = half * TILE_SIZE + 1
    count_high, count_low = (masks[:, first + i * blocks : first + (i + 1) * blocks].astype(f32) for i in range(2))
    all_inverse = (1.0 / jnp.maximum(count_high * TILE_SIZE + count_low, 1.0)).reshape(planes, rows)
    p0 = partial_of(0, tile_ids)

    p0, cot_end, cot_far, ids = gated((p0, cot_end, cot_far, tile_ids), (cot_s, cot_xs, all_inverse))
    a0 = to_middle(p0)
    cot_end_x = swap_x(cot_end)
    p1, p2, p3 = (partial_of(group, ids) for group in range(1, planes))
    cot_end_s, cot_far_s = swap_core(cot_end), swap_core(cot_far)
    cot_end, p1, p2, p3 = gated((cot_end, p1, p2, p3), ())
    cot_far_end = across(cot_end)

    p1, p0, a0, cot_far, r01, cot_end_x = gated((p1, p0, a0, cot_far, r01, cot_end_x), (cot_end_s, cot_far_s))
    a1 = to_middle(p1)
    s0 = both(p0, a0)
    o0 = across(s0)
    cot_far_x = swap_x(cot_far)
    y01 = swap_y(r01)
    cot_end_xs = swap_core(cot_end_x)

    p2, p1, a1, cot_far_x, cot_far_end = gated((p2, p1, a1, cot_far_x, cot_far_end), (cot_end_xs, y01))
    a2 = to_middle(p2)
    s1 = both(p1, a1)
    o1 = across(s1)
    cot_far_end_x = swap_x(cot_far_end)
    cot_far_xs, cot_far_end_s = swap_core(cot_far_x), swap_core(cot_far_end)

    f0 = mixed_of(0, s0, o0)
    p3, p2, a2, f0, cot_far_end_x = gated((p3, p2, a2, f0, cot_far_end_x), (cot_far_xs, cot_far_end_s))
    f0_x = swap_x(f0)
    a3 = to_middle(p3)
    s2 = both(p2, a2)
    o2 = across(s2)
    f0_s, cot_far_end_xs = swap_core(f0), swap_core(cot_far_end_x)

    f1 = mixed_of(1, s1, o1)
    f1, f0_x = gated((f1, f0_x), (f0_s, cot_far_end_xs))
    f1_x = swap_x(f1)
    p3, a3, own01 = gated((p3, a3, own01), ())
    e01 = to_middle(own01)
    s3 = both(p3, a3)
    o3 = across(s3)
    f1_s, f0_xs = swap_core(f1), swap_core(f0_x)

    f2 = mixed_of(2, s2, o2)
    f2, f1_x = gated((f2, f1_x), (f1_s, f0_xs))
    f2_x = swap_x(f2)
    e01, o2 = gated((e01, o2), ())
    r_e01 = across(e01)
    ye01 = swap_y(e01)
    f2_s, f1_xs = swap_core(f2), swap_core(f1_x)

    f3 = mixed_of(3, s3, o3)
    f3, f2_x, own23 = gated((f3, f2_x, own23), (f2_s, f1_xs, ye01))
    f3_x = swap_x(f3)
    e23 = to_middle(own23)
    f3_s, f2_xs = swap_core(f3), swap_core(f2_x)
    r_e01, f3_s = gated((r_e01, f3_s), (f2_xs,))
    y_e01 = swap_y(r_e01)

    f3_x, y_e01 = gated((f3_x, y_e01), (f3_s,))
    f3_xs = swap_core(f3_x)
    r2 = across(jnp.stack([own23[0], e23[0]]))
    r3 = across(jnp.stack([own23[1], e23[1]]))
    ye23 = swap_y(e23)
    features = [[f0, f0_s, f0_x, f0_xs], [f1, f1_s, f1_x, f1_xs], [f2, f2_s, f2_x, f2_xs], [f3, f3_s, f3_x, f3_xs]]
    cotangents = [
        [cot, cot_s, cot_x, cot_xs],
        [cot_end, cot_end_s, cot_end_x, cot_end_xs],
        [cot_far_end, cot_far_end_s, cot_far_end_x, cot_far_end_xs],
        [cot_far, cot_far_s, cot_far_x, cot_far_xs],
    ]
    scalars = jnp.stack([plane ^ column, part, plane]).astype(jnp.int32)
    bias = b_in.reshape(1, -1)

    def run(chunk, *moved):
        return hidden_chunk(chunk, scalars, features, cotangents, (w_in, w_out_t), *moved, bias)

    g0 = run(0, [(r01, 0), (r_e01, 0), (e01, 0), (y01, 0), (y_e01, 0), (ye01, 0)])

    r2, end0 = gated((r2, g0[2]), ())
    y2 = swap_y(r2)
    c0 = to_end(end0)
    g1 = run(1, [(r01, 1), (r_e01, 1), (e01, 1), (y01, 1), (y_e01, 1), (ye01, 1)])

    r3, y2, end1, c0 = gated((r3, y2, g1[2], c0), (ye23,))
    y3 = swap_y(r3)
    c1 = to_end(end1)
    g2 = run(2, [(r2, 0), (r2, 1), (e23, 0), (y2, 0), (y2, 1), (ye23, 0)])

    y3, end2, c1 = gated((y3, g2[2], c1), ())
    c2 = to_end(end2)
    g3 = run(3, [(r3, 0), (r3, 1), (e23, 1), (y3, 0), (y3, 1), (ye23, 1)])
    end3, c0, c1, c2 = gated((g3[2], c0, c1, c2), ())
    c3 = to_end(end3)

    is_middle = (plane == 1) | (plane == 2)
    grad_w_in = jnp.zeros((width, hidden_units), f32)
    grad_w_out = jnp.zeros((hidden_units, width), f32)
    biases = []
    for chunk, ((own_in, own_out, _, own_bias), end) in enumerate(zip((g0, g1, g2, g3), (c0, c1, c2, c3))):
        end = end.astype(f32)
        here = slice(chunk * size, (chunk + 1) * size)
        end_out = end[width : 2 * width].reshape(width // size, size, size).transpose(1, 0, 2).reshape(size, width)
        grad_w_in = grad_w_in.at[:, here].set(jnp.where(is_middle, own_in, end[:width]))
        grad_w_out = grad_w_out.at[here].set(jnp.where(is_middle, own_out, end_out))
        high, middle, low = (end[2 * width + i] for i in range(3))
        biases.append(jnp.where(is_middle, own_bias[0], (high + middle) + low))
    return (grad_w_in, grad_w_out, jnp.concatenate(biases))


def gathered(previous_embedding, tile_source, tile_mask, row_order, w_in, b_in, w_out, grad_out):
    groups = lax.axis_size("vocab")
    blocks, slots_per = tile_source.shape
    tiles_here = previous_embedding.shape[0] // TILE_SIZE
    columns = previous_embedding.shape[1]
    flat_source = tile_source.reshape(-1)
    owner_dev = flat_source // tiles_here
    local_tile = flat_source % tiles_here
    total_slots = flat_source.shape[0]
    capacity = max(2, 2 * total_slots // groups)
    slot_ids = jnp.arange(total_slots)
    earlier = slot_ids[None, :] < slot_ids[:, None]
    same_owner = owner_dev[None, :] == owner_dev[:, None]
    position = jnp.sum(jnp.where(earlier & same_owner, 1, 0), axis=1).astype(jnp.int32)
    owner_hit = owner_dev[:, None] == jnp.arange(groups)[None, :]
    place_hit = position[:, None] == jnp.arange(capacity)[None, :]
    placed = owner_hit[:, :, None] & place_hit[:, None, :]
    slot_index = owner_dev * capacity + position
    mask_values = tile_mask.astype(jnp.bfloat16)
    requests = jnp.sum(jnp.where(placed, local_tile[:, None, None], 0), axis=0)
    tile_lookup = previous_embedding.reshape(tiles_here, TILE_SIZE, columns)
    found_tiles = jnp.take(
        tile_lookup,
        lax.all_to_all(requests, "vocab", split_axis=0, concat_axis=0, tiled=True),
        axis=0,
    )
    arrived = lax.all_to_all(found_tiles, "vocab", split_axis=0, concat_axis=0, tiled=True)
    picked = arrived.reshape(groups * capacity, TILE_SIZE, columns)[slot_index]
    picked = picked.reshape(blocks, slots_per, TILE_SIZE, columns)
    summed = jnp.einsum("bkrc,bkcd->brd", mask_values, picked, preferred_element_type=jnp.float32)
    counts = jnp.sum(tile_mask, axis=(1, 3))
    inverse = 1.0 / jnp.maximum(counts, 1).astype(jnp.float32)
    mixed = (summed * inverse[:, :, None]).astype(jnp.bfloat16).reshape(blocks * TILE_SIZE, columns)
    rows_here = mixed.shape[0]
    ordered = mixed[row_order % rows_here]
    w_in_full = lax.all_gather(w_in, "vocab", axis=0, tiled=True)
    features = lax.all_gather(ordered, ("mp", "sub"), axis=1, tiled=True)
    preact = jnp.dot(features, w_in_full, preferred_element_type=jnp.float32) + b_in
    activation, act_slope = gelu_parts(preact)
    hidden = activation.astype(jnp.bfloat16)
    w_out_full = lax.all_gather(w_out, "vocab", axis=1, tiled=True)
    cotangent = lax.all_gather(grad_out, ("mp", "sub"), axis=1, tiled=True)
    hidden_grad = lax.dot_general(
        cotangent, w_out_full, (((1,), (1,)), ((), ())), preferred_element_type=jnp.float32
    )
    pre_grad = (hidden_grad * act_slope).astype(jnp.bfloat16)
    grad_bias = lax.psum(jnp.sum(pre_grad.astype(jnp.float32), axis=0), "vocab")
    grad_w_in = lax.psum_scatter(
        lax.dot_general(
            features, pre_grad, (((0,), (0,)), ((), ())), preferred_element_type=jnp.float32
        ).astype(jnp.bfloat16),
        "vocab",
        scatter_dimension=0,
        tiled=True,
    ).astype(jnp.float32)
    grad_w_out = (
        lax.psum_scatter(
            lax.dot_general(
                cotangent, hidden, (((0,), (0,)), ((), ())), preferred_element_type=jnp.float32
            ).astype(jnp.bfloat16),
            "vocab",
            scatter_dimension=0,
            tiled=True,
        )
        .astype(jnp.float32)
        .T
    )
    return (grad_w_in, grad_w_out, grad_bias)


def solution(mesh):
    placed = (
        P("vocab", ("mp", "sub")),
        P(("groups", "vocab"), None),
        P(("groups", "vocab"), None, None, None),
        P(("groups", "vocab")),
        P("vocab", ("mp", "sub")),
        P(("mp", "sub")),
        P(("mp", "sub"), "vocab"),
        P(("groups", "vocab"), ("mp", "sub")),
    )
    return jax.shard_map(
        middle_planes if planes_fit(mesh) else gathered,
        mesh=mesh,
        in_specs=placed,
        out_specs=(
            P(("groups", "vocab"), ("mp", "sub")),
            P(("groups", "mp", "sub"), "vocab"),
            P(("groups", "mp", "sub")),
        ),
        check_vma=False,
    )
```
